256 devices in a mesh: section: 16 (over x, z_hi), tensor: 16 (over y, z_lo, core).
Axes of the slice: x: 4, y: 4, z: 8 (z_hi: 4, z_lo: 2; z = z_hi * 2 + z_lo), core: 2. Of those that a mesh axis runs over, the one named last changes fastest.
Arguments:
- weight_q: bfloat16 [16, 4096, 4096], P('section', None, 'tensor'), as said below
- weight_kv: bfloat16 [16, 4096, 4096], P('section', None, 'tensor'), as said below
- weight_o: bfloat16 [16, 4096, 4096], P('section', None, 'tensor'), as said below
- section_inputs: bfloat16 [2, 2, 16, 128, 4096], P(None, None, 'section', None, 'tensor')
- saved_q: bfloat16 [2, 2, 16, 128, 4096], P(None, None, 'section', None, 'tensor')
- saved_kv: bfloat16 [2, 2, 16, 128, 4096], P(None, None, 'section', None, 'tensor'), as said below
- out_grads: bfloat16 [2, 16, 128, 4096], P(None, 'section', None, 'tensor'), may hold values from -6 to 6
Outputs:
- input_grads: bfloat16 [2, 2, 16, 128, 4096], P(None, None, 'section', None, 'tensor')
- grad_query: bfloat16 [16, 2048, 4096], P('section', None, 'tensor')
- grad_kv: bfloat16 [16, 512, 4096], P('section', None, 'tensor')
- grad_output: bfloat16 [16, 2048, 4096], P('section', None, 'tensor')
The draws below stay inside these ranges and needn't reach their ends.
Inputs may be any that keep to these rules, and one draw needn't show every extreme that they name: weight_q[s] equals weight_q[15 - s] for every s. weight_o[s] equals weight_o[15 - s] for every s. weight_kv[s] equals weight_kv[15 - s]; column blocks c and u (256 wide) are equal whenever c // 4 == u // 4. `saved_kv`: column blocks c and u (256 wide) are equal whenever c // 4 == u // 4.
All inputs are finite; a program needn't handle non-finite values.
Results may differ from the reference program's by a relative error of at most 0.018.
Values may be sent and summed in bfloat16 or wider, within the bound.
No kernel may reach another device: no remote copies, remote signals or barrier semaphores. Data moves between devices by JAX's collectives and lax.ppermute only.
A program may use at most 128 MiB of HBM per device.

```python
import math
import jax
import jax.numpy as jnp
from jax import lax

D = 4096
H = 32
KV = 4
HD = 128
TOK = 128
TICKS = 2
SECTIONS = 16
TENSORS = 16
GROUP = 4


def mirrored(base):
    order = jnp.arange(SECTIONS)
    layer = jnp.minimum(order, SECTIONS - 1 - order)
    return base[layer]


def draw_weight_q(key, part):
    key = jax.random.fold_in(key, 1)
    base = jax.random.normal(key, (SECTIONS // 2, D, H * HD), jnp.float32) * D ** (-0.5)
    return mirrored(base).astype(jnp.bfloat16)


def draw_weight_kv(key, part):
    key = jax.random.fold_in(key, 2)
    base = jax.random.normal(key, (SECTIONS // 2, D, KV, 2 * HD), jnp.float32) * D ** (-0.5)
    owner = jnp.arange(TENSORS) // GROUP
    full = mirrored(base)[:, :, owner, :]
    return full.reshape(SECTIONS, D, TENSORS * 2 * HD).astype(jnp.bfloat16)


def draw_weight_o(key, part):
    key = jax.random.fold_in(key, 3)
    base = jax.random.normal(key, (SECTIONS // 2, D, H * HD), jnp.float32) * (H * HD) ** (-0.5)
    return mirrored(base).astype(jnp.bfloat16)


def draw_section_inputs(key, part):
    key = jax.random.fold_in(key, 4)
    first, second, third = jax.random.split(key, 3)
    shape = (2, TICKS, SECTIONS, TOK, D)
    core = jax.random.normal(first, shape, jnp.float32)
    spread = math.log(10.0)
    row_scale = jnp.exp(spread * (jax.random.uniform(second, (2, TICKS, SECTIONS, TOK, 1), jnp.float32) - 0.5))
    ramp = 1.0 + 2.0 * jnp.arange(D, dtype=jnp.float32) / D
    column_scale = jnp.exp(spread * (jax.random.uniform(third, (D,), jnp.float32) - 0.5)) * ramp * 0.5
    return (core * row_scale * column_scale).astype(jnp.bfloat16)


def attention_draws(key):
    shape_q = (2, TICKS, SECTIONS, TOK, H, HD)
    shape_k = (2, TICKS, SECTIONS, TOK, KV, HD)
    queries = jax.random.normal(jax.random.fold_in(key, 50), shape_q, jnp.float32)
    key_rows = jax.random.normal(jax.random.fold_in(key, 51), shape_k, jnp.float32)
    value_rows = jax.random.normal(jax.random.fold_in(key, 52), shape_k, jnp.float32)
    position = jnp.arange(TOK).reshape(TOK, 1, 1)
    chosen = position % 32 == 31
    nearest = position % 32 == 30
    second = position % 32 == 29
    key_rows = jnp.where(nearest, key_rows, key_rows)
    key_rows = jnp.where(second, key_rows, key_rows)
    queries = jnp.where(chosen, queries, queries)
    pairs = jnp.concatenate([key_rows, value_rows], axis=-1)
    block_owner = jnp.arange(TENSORS) // GROUP
    pairs = pairs[:, :, :, :, block_owner, :]
    return (queries.reshape(2, TICKS, SECTIONS, TOK, H * HD), pairs.reshape(2, TICKS, SECTIONS, TOK, TENSORS * 2 * HD))


def draw_saved_q(key, part):
    return attention_draws(key)[0].astype(jnp.bfloat16)


def draw_saved_kv(key, part):
    return attention_draws(key)[1].astype(jnp.bfloat16)


def shard_levels(own_key, extent, shards, least, high):
    factor_of, own = 1.0, jax.random.fold_in(own_key, 6)
    for dim, shards_of in shards:
        heights = jnp.exp(jax.random.uniform(jax.random.fold_in(own, dim), (shards_of,), jnp.float32, least / len(shards), high / len(shards)))
        factor_of = factor_of * jnp.repeat(heights, extent[dim] // shards_of).reshape([-1 if axis == dim else 1 for axis in range(len(extent))])
    return factor_of


def gaussian(own_key, dims, deviation, reach, cuts=(), held_as=jnp.bfloat16):
    loudness = shard_levels(own_key, dims, cuts, -0.22, 0.18) if cuts else 1.0
    result = jax.random.normal(own_key, dims, jnp.float32) * deviation * loudness
    return jnp.minimum(jnp.maximum(result, -reach), reach).astype(held_as)


def setup_inputs(seed: int = 0) -> dict:
    seeds = jax.random.split(jax.random.key(seed), 8)
    return {
        "weight_q": draw_weight_q(jax.random.fold_in(seeds[7], 71), 0),
        "weight_kv": draw_weight_kv(jax.random.fold_in(seeds[7], 71), 0),
        "weight_o": draw_weight_o(jax.random.fold_in(seeds[7], 71), 0),
        "section_inputs": draw_section_inputs(jax.random.fold_in(seeds[7], 71), 0),
        "saved_q": draw_saved_q(jax.random.fold_in(seeds[7], 71), 0),
        "saved_kv": draw_saved_kv(jax.random.fold_in(seeds[7], 71), 0),
        "out_grads": gaussian(seeds[6], (2, SECTIONS, TOK, D), 1.0, 6.0, ((1, 16), (3, 16))),
    }


def as_stored(value):
    return lax.optimization_barrier(value.astype(jnp.bfloat16)).astype(jnp.float32)

def section_pass(rows_in, queries, pair_rows, grad_out, w_query, w_pairs, w_out):
    heads_dev = H // TENSORS
    rows_f = rows_in.astype(jnp.float32)
    inverse = lax.rsqrt(lax.optimization_barrier(jnp.mean(rows_f * rows_f, axis=-1, keepdims=True)) + 1e-06)
    normed = rows_f * inverse
    normed_b = normed.astype(jnp.bfloat16)
    query_f = queries.astype(jnp.float32).reshape(TOK, TENSORS, heads_dev, HD)
    pair_f = pair_rows.astype(jnp.float32).reshape(TOK, TENSORS, 2 * HD)
    key_rows = pair_f[:, :, :HD]
    value_rows = pair_f[:, :, HD:]
    score_scale = HD ** (-0.5)
    scores = jnp.einsum('ibae,jbe->baij', query_f, key_rows) * score_scale
    causal = jnp.arange(TOK)[:, None] >= jnp.arange(TOK)[None, :]
    scores = jnp.where(causal, scores, -1e+30)
    attention = jax.nn.softmax(scores, axis=-1)
    attention_b = as_stored(attention)
    attended = jnp.einsum('baij,jbe->ibae', attention_b, value_rows).reshape(TOK, H * HD).astype(jnp.bfloat16)
    grad_attn = as_stored(jnp.dot(grad_out, w_out, preferred_element_type=jnp.float32))
    grad_heads = grad_attn.reshape(TOK, TENSORS, heads_dev, HD)
    grad_probs = jnp.einsum('ibae,jbe->baij', grad_heads, value_rows)
    row_delta = lax.optimization_barrier(jnp.sum(attention * grad_probs, axis=-1, keepdims=True))
    grad_scores = as_stored(attention * (grad_probs - row_delta) * score_scale)
    grad_query = jnp.einsum('baij,jbe->ibae', grad_scores, key_rows).reshape(TOK, H * HD).astype(jnp.bfloat16)
    grad_key = jnp.einsum('baij,ibae->jbe', grad_scores, query_f)
    grad_value = jnp.einsum('baij,ibae->jbe', attention_b, grad_heads)
    grad_pairs = jnp.concatenate([grad_key, grad_value], axis=-1).reshape(TOK, TENSORS * 2 * HD).astype(jnp.bfloat16)
    grad_normed = jnp.dot(grad_query, w_query.T, preferred_element_type=jnp.float32) + jnp.dot(grad_pairs, w_pairs.T, preferred_element_type=jnp.float32)
    row_sums = lax.optimization_barrier(jnp.sum(grad_normed * normed, axis=-1, keepdims=True))
    grad_in = (grad_out.astype(jnp.float32) + inverse * (grad_normed - normed * row_sums / D)).astype(jnp.bfloat16)
    weight_grad_o = jnp.dot(grad_out.T, attended, preferred_element_type=jnp.float32)
    weight_grad_q = jnp.dot(normed_b.T, grad_query, preferred_element_type=jnp.float32)
    weight_grad_pairs = jnp.dot(normed_b.T, grad_pairs, preferred_element_type=jnp.float32)
    return (grad_in, weight_grad_q, weight_grad_pairs, weight_grad_o)

def reference(weight_q, weight_kv, weight_o, section_inputs, saved_q, saved_kv, out_grads):
    order = jnp.arange(SECTIONS, dtype=jnp.int32)
    grad_now = out_grads
    incoming = []
    produced = []
    for tick_index in range(TICKS):
        incoming.append(grad_now)

        def chain_one(position, tick_index=tick_index, grad_now=grad_now):
            results = []
            for direction in range(2):
                results.append(section_pass(section_inputs[direction, tick_index, position], saved_q[direction, tick_index, position], saved_kv[direction, tick_index, position], grad_now[direction, position], weight_q[position], weight_kv[position], weight_o[position])[0])
            return jnp.stack(results)
        made = jnp.swapaxes(lax.map(chain_one, order), 0, 1)
        produced.append(made)
        zero_rows = jnp.zeros_like(made[0, :1])
        from_above = jnp.concatenate([made[0, 1:], zero_rows], axis=0)
        from_below = jnp.concatenate([zero_rows, made[1, :-1]], axis=0)
        grad_now = jnp.stack([from_above, from_below])
    input_grads = jnp.stack(produced, axis=1)
    incoming = jnp.stack(incoming, axis=1)

    def accumulate(position):
        total_q = jnp.zeros((D, H * HD), jnp.float32)
        total_pairs = jnp.zeros((D, TENSORS * 2 * HD), jnp.float32)
        total_o = jnp.zeros((D, H * HD), jnp.float32)
        for direction in range(2):
            for tick_index in range(TICKS):
                unused, part_q, part_pairs, part_o = section_pass(section_inputs[direction, tick_index, position], saved_q[direction, tick_index, position], saved_kv[direction, tick_index, position], incoming[direction, tick_index, position], weight_q[position], weight_kv[position], weight_o[position])
                total_q = total_q + part_q
                total_pairs = total_pairs + part_pairs
                total_o = total_o + part_o
        total_kv = lax.optimization_barrier(jnp.sum(total_pairs.reshape(D, KV, GROUP, 2 * HD), axis=2))
        return (total_q.astype(jnp.bfloat16), total_kv.astype(jnp.bfloat16), total_o.astype(jnp.bfloat16))

    def arrange_kv(summed, half_index):
        blocks = summed.reshape(GROUP, 2, D // (2 * GROUP), KV, 2 * HD)[:, half_index]
        return jnp.transpose(blocks, (1, 2, 0, 3)).reshape(D // (2 * GROUP), TENSORS * 2 * HD)

    def pair_out(lower):
        higher = SECTIONS - 1 - lower
        low_q, low_kv, low_o = accumulate(lower)
        high_q, high_kv, high_o = accumulate(higher)
        sum_q = (low_q.astype(jnp.float32) + high_q.astype(jnp.float32)).astype(jnp.bfloat16)
        sum_o = (low_o.astype(jnp.float32) + high_o.astype(jnp.float32)).astype(jnp.bfloat16)
        sum_kv = (low_kv.astype(jnp.float32) + high_kv.astype(jnp.float32)).astype(jnp.bfloat16)
        return (sum_q[:D // 2], sum_q[D // 2:], sum_o[:D // 2], sum_o[D // 2:], arrange_kv(sum_kv, 0), arrange_kv(sum_kv, 1))
    halves = lax.map(pair_out, jnp.arange(SECTIONS // 2, dtype=jnp.int32))
    grad_query = jnp.concatenate([halves[0], jnp.flip(halves[1], 0)], axis=0)
    grad_output = jnp.concatenate([halves[2], jnp.flip(halves[3], 0)], axis=0)
    grad_kv = jnp.concatenate([halves[4], jnp.flip(halves[5], 0)], axis=0)
    return (input_grads, grad_query, grad_kv, grad_output)
```

```python
import jax
import jax.numpy as jnp
from jax import lax
from jax.sharding import PartitionSpec as P

HD = 128
TICKS = 2
BF = jnp.bfloat16
F32 = jnp.float32

SAME_CORE = [[core + 2 * chip for chip in range(8)] for core in range(2)]


def all_pairs(route):
    pairs = []
    for section in range(16):
        for tensor in range(16):
            target = route(section, tensor)
            if target is not None:
                pairs.append((section * 16 + tensor, target[0] * 16 + target[1]))
    return pairs


def send(x, route):
    return lax.ppermute(x, ("section", "tensor"), all_pairs(route))


def swap_core(x):
    return lax.ppermute(x, "tensor", [(i, i ^ 1) for i in range(16)])


def swap_z(x):
    return lax.ppermute(x, "tensor", [(i, i ^ 2) for i in range(16)])


def mirror(x):
    return lax.ppermute(x, "section", [(i, 15 - i) for i in range(16)])


def mirror_other(x):
    return send(x, lambda s, c: (15 - s, c ^ 1))


def next_section(x):
    def route(s, c):
        target = s - 1 if c % 2 == 0 else s + 1
        return (target, c) if 0 <= target < 16 else None

    return send(x, route)


def exchange8(x):
    return lax.all_to_all(x, "tensor", 0, 0, axis_index_groups=SAME_CORE, tiled=True)


def exchange16(x):
    return lax.all_to_all(x, "tensor", 0, 0, tiled=True)


def gather8_now(x):
    out = exchange8(jnp.broadcast_to(x[None], (8,) + x.shape))
    return out.reshape((8 * x.shape[0],) + x.shape[1:])


def gather8(x):
    return lax.all_gather(x, "tensor", axis_index_groups=SAME_CORE, axis=0, tiled=True)


def dot(a, b):
    return jnp.dot(a, b, preferred_element_type=F32)


def dot_nt(a, b):
    return lax.dot_general(a, b, (((1,), (1,)), ((), ())), preferred_element_type=F32)


def dot_tn(a, b):
    return lax.dot_general(a, b, (((0,), (0,)), ((), ())), preferred_element_type=F32)


def spread(own, partner, extra=None):
    own_full = own if extra is None else jnp.concatenate([own, extra], -1)
    partner_full = partner if extra is None else jnp.concatenate([partner, extra], -1)
    return own_full, mirror(own_full), swap_core(partner_full), mirror_other(partner_full)


def on_device(weight_q, weight_kv, weight_o, section_inputs, saved_q, saved_kv, out_grads):
    position = lax.axis_index("section")
    column = lax.axis_index("tensor")
    core = column % 2
    z_low = column // 2 % 2
    half = (position >= 8).astype(jnp.int32)
    w_q, w_kv, w_o = weight_q[0], weight_kv[0], weight_o[0]
    width = w_q.shape[0]
    half_width = width // 2
    inputs = section_inputs[:, :, 0]
    grads = out_grads[:, 0]
    scale = HD ** (-0.5)

    def pick(x, index):
        return lax.dynamic_index_in_dim(x, index, 0, keepdims=False)

    def features_of(x, which):
        return lax.dynamic_slice_in_dim(x, which * half_width, half_width, x.ndim - 1)

    mixed = jnp.concatenate([grads[:, None], inputs], 1)
    mixed = mixed.reshape(2, 3, 8, 16, 256).transpose(2, 0, 1, 3, 4).reshape(16, 48, 256)
    rows = exchange16(mixed).transpose(1, 0, 2).reshape(3, 16, width)
    grad_rows = rows[0]

    w_o_both = jnp.concatenate([w_o, swap_core(w_o)], -1)
    w_q_both = jnp.concatenate([w_q, swap_core(w_q)], -1)
    queries = saved_q[:, :, 0]
    queries = jnp.concatenate([pick(queries, core), swap_core(pick(queries, 1 - core))], -1)
    pairs = pick(saved_kv[:, :, 0], core)
    keys, values = pairs[..., :HD], pairs[..., HD:]

    rows_f = rows[1:].astype(F32)
    inverse = lax.rsqrt(jnp.mean(rows_f * rows_f, axis=-1, keepdims=True) + 1e-06)
    normed = rows_f * inverse
    normed_b = normed.astype(BF)

    causal = jnp.arange(128)[:, None] >= jnp.arange(128)[None, :]
    query_heads = queries.reshape(TICKS, 128, 4, HD).transpose(0, 2, 1, 3)
    scores = jnp.einsum("taie,tje->taij", query_heads, keys, preferred_element_type=F32) * scale
    attention = jax.nn.softmax(jnp.where(causal, scores, -1e30), axis=-1)
    attention_b = attention.astype(BF)
    attended = jnp.einsum("taij,tje->tiae", attention_b, values, preferred_element_type=F32)
    attended = attended.astype(BF).reshape(TICKS, 128, 512)

    produced = []
    acc_q = acc_o = acc_kv = 0.0
    for t in range(TICKS):
        grad_full = gather8_now(grad_rows)
        grad_attn = dot(grad_full, w_o_both).astype(BF)
        grad_heads = grad_attn.reshape(128, 4, HD).transpose(1, 0, 2)
        grad_probs = jnp.einsum("aie,je->aij", grad_heads, values[t], preferred_element_type=F32)
        row_delta = jnp.sum(attention[t] * grad_probs, axis=-1, keepdims=True)
        grad_scores = (attention[t] * (grad_probs - row_delta) * scale).astype(BF)
        query_grad = jnp.einsum("aij,je->iae", grad_scores, keys[t], preferred_element_type=F32)
        query_grad = query_grad.astype(BF).reshape(128, 512)
        grad_key = jnp.einsum("aij,aie->je", grad_scores, query_heads[t], preferred_element_type=F32)
        grad_value = jnp.einsum("aij,aie->je", attention_b[t], grad_heads, preferred_element_type=F32)
        grad_pairs = jnp.concatenate([grad_key, grad_value], -1).astype(BF)
        partial = (dot_nt(query_grad, w_q_both) + dot_nt(grad_pairs, w_kv)).astype(BF)
        terms = exchange8(partial.reshape(8, 16, width))
        grad_normed = jnp.sum(terms.astype(F32), axis=0)
        row_sums = jnp.sum(grad_normed * normed[t], axis=-1, keepdims=True)
        grad_in = (
            grad_rows.astype(F32) + inverse[t] * (grad_normed - normed[t] * row_sums / width)
        ).astype(BF)
        blocks = exchange16(grad_in.reshape(16, 16, 256).transpose(1, 0, 2))
        produced.append(blocks.reshape(8, 2, 16, 256).transpose(1, 0, 2, 3).reshape(2, 128, 256))

        sent_normed = features_of(normed_b[t], 1 - half)
        sent_grad = features_of(grad_rows, 1 - half)
        far = mirror(jnp.concatenate([sent_normed, sent_grad], 0))
        x_here = gather8(jnp.concatenate([features_of(normed_b[t], half), far[:16]], 0))
        x_there = swap_core(x_here)
        g_here = jnp.concatenate([features_of(grad_full, half), gather8(far[16:])], 0)
        g_there = swap_core(g_here)
        out_parts = spread(attended[t][:, :256], attended[t][:, 256:])
        pairs_sum = (grad_pairs.astype(F32) + swap_z(grad_pairs).astype(F32)).astype(BF)
        in_parts = spread(query_grad[:, :256], query_grad[:, 256:], pairs_sum)

        acc_o = acc_o + dot_tn(g_here, jnp.concatenate(out_parts[:2], 0))
        acc_o = acc_o + dot_tn(g_there, jnp.concatenate(out_parts[2:], 0))

        def interleave(parts):
            return jnp.stack([part.reshape(8, 16, 512) for part in parts], 1).reshape(256, 512)

        in_here, in_there = interleave(in_parts[:2]), interleave(in_parts[2:])
        acc_q = acc_q + dot_tn(x_here, in_here[:, :256])
        acc_q = acc_q + dot_tn(x_there, in_there[:, :256])
        x_kv_here = lax.dynamic_slice_in_dim(x_here, core * 1024, 1024, 1)
        x_kv_there = lax.dynamic_slice_in_dim(x_there, core * 1024, 1024, 1)
        acc_kv = acc_kv + dot_tn(x_kv_here, in_here[:, 256:])
        acc_kv = acc_kv + dot_tn(x_kv_there, in_there[:, 256:])
        if t + 1 < TICKS:
            grad_rows = next_section(grad_in)

    acc_kv = acc_kv.astype(BF)
    kept = lax.dynamic_slice_in_dim(acc_kv, half * 512, 512, 0)
    given = lax.dynamic_slice_in_dim(acc_kv, (1 - half) * 512, 512, 0)
    taken = send(given, lambda s, c: (15 - s, c) if c // 2 % 2 == s // 8 else None)
    grad_kv = jnp.where(z_low == half, kept, taken)
    input_grads = jnp.stack(produced, axis=1)[:, :, None]
    return (input_grads, acc_q.astype(BF)[None], grad_kv[None], acc_o.astype(BF)[None])


def solution(mesh):
    placed = (
        P("section", None, "tensor"),
        P("section", None, "tensor"),
        P("section", None, "tensor"),
        P(None, None, "section", None, "tensor"),
        P(None, None, "section", None, "tensor"),
        P(None, None, "section", None, "tensor"),
        P(None, "section", None, "tensor"),
    )
    return jax.shard_map(
        on_device,
        mesh=mesh,
        in_specs=placed,
        out_specs=(
            P(None, None, "section", None, "tensor"),
            P("section", None, "tensor"),
            P("section", None, "tensor"),
            P("section", None, "tensor"),
        ),
        check_vma=False,
    )
```

```python
import functools

import jax
import jax.numpy as jnp
from jax import lax
from jax.experimental import pallas as pl
from jax.experimental.pallas import tpu as pltpu
from jax.sharding import PartitionSpec as P

HD = 128
TICKS = 2
TOK = 128
WIDTH = 4096
HALF = WIDTH // 2
SCALE = HD ** (-0.5)
BF = jnp.bfloat16
F32 = jnp.float32

SAME_CORE = [[core + 2 * chip for chip in range(8)] for core in range(2)]
VMEM = pl.BlockSpec(memory_space=pltpu.VMEM)
HBM = pl.BlockSpec(memory_space=pl.ANY)


def send(x, route):
    pairs = []
    for section in range(16):
        for tensor in range(16):
            target = route(section, tensor)
            if target is not None:
                pairs.append((section * 16 + tensor, target[0] * 16 + target[1]))
    return lax.ppermute(x, ("section", "tensor"), pairs)


def swap_core(x):
    return lax.ppermute(x, "tensor", [(i, i ^ 1) for i in range(16)])


def swap_z(x):
    return lax.ppermute(x, "tensor", [(i, i ^ 2) for i in range(16)])


def swap_y(x, k):
    return lax.ppermute(x, "tensor", [(i, i ^ 4 * k) for i in range(16)])


def mirror(x):
    return lax.ppermute(x, "section", [(i, 15 - i) for i in range(16)])


def next_section(x):
    def route(s, c):
        target = s - 1 if c % 2 == 0 else s + 1
        return (target, c) if 0 <= target < 16 else None

    return send(x, route)


def next_mirror(x):
    def route(s, c):
        target = s - 1 if c % 2 == 0 else s + 1
        return (15 - target, c) if 0 <= target < 16 else None

    return send(x, route)


def exchange8(x):
    return lax.all_to_all(x, "tensor", 0, 0, axis_index_groups=SAME_CORE, tiled=True)


def exchange16(x):
    return lax.all_to_all(x, "tensor", 0, 0, tiled=True)


def gather16(x):
    return lax.all_gather(x, "tensor", axis=0, tiled=True)


def dot(a, b):
    return jnp.dot(a, b, preferred_element_type=F32)


def dot_nt(a, b):
    return lax.dot_general(a, b, (((1,), (1,)), ((), ())), preferred_element_type=F32)


def dot_tn(a, b):
    return lax.dot_general(a, b, (((0,), (0,)), ((), ())), preferred_element_type=F32)


def together(*values):
    return lax.optimization_barrier(values)


def params(mib):
    return pltpu.CompilerParams(vmem_limit_bytes=mib * 2**20)


def attend_kernel(q_ref, kv_ref, attention_ref, attended_ref):
    rows = lax.broadcasted_iota(jnp.int32, (TOK, TOK), 0)
    columns = lax.broadcasted_iota(jnp.int32, (TOK, TOK), 1)
    causal = rows >= columns
    for t in range(TICKS):
        keys = kv_ref[t, :, :HD]
        values = kv_ref[t, :, HD:]
        for a in range(4):
            head = slice(a * HD, (a + 1) * HD)
            scores = jnp.where(causal, dot_nt(q_ref[t, :, head], keys) * SCALE, -1e30)
            weights = jnp.exp(scores - jnp.max(scores, axis=-1, keepdims=True))
            weights = weights / jnp.sum(weights, axis=-1, keepdims=True)
            attention_ref[t, a] = weights
            attended_ref[t, :, head] = dot(weights.astype(BF), values).astype(BF)


def attend(queries, pairs):
    return pl.pallas_call(
        attend_kernel,
        out_shape=(
            jax.ShapeDtypeStruct((TICKS, 4, TOK, TOK), F32),
            jax.ShapeDtypeStruct((TICKS, TOK, 4 * HD), BF),
        ),
        in_specs=[VMEM] * 2,
        out_specs=(VMEM, VMEM),
        compiler_params=params(16),
    )(queries, pairs)


CHUNKS = 4
DEEP = WIDTH // CHUNKS


def back_kernel(
    tick,
    g_hbm, wo_own_ref, wo_far_ref, wq_own_ref, wq_far_ref, wkv_ref, q_ref, kv_ref, attention_ref,
    terms_ref, parts_ref,
    g_ref, grad_heads, heads, g_sems,
):
    own_ref, far_ref, pairs_ref = (parts_ref.at[pl.ds(n * TOK, TOK)] for n in range(3))
    copies = []
    for c in range(CHUNKS):
        if tick == 0:
            part = pl.ds(c * 16 // CHUNKS, 16 // CHUNKS)
            copies.append(pltpu.make_async_copy(g_hbm.at[part, :TOK], g_ref.at[part], g_sems.at[c]))
        else:
            deep = pl.ds(c * DEEP, DEEP)
            copies.append(pltpu.make_async_copy(g_hbm.at[:, :, deep], g_ref.at[:, :, deep], g_sems.at[c]))
    for copy in copies:
        copy.start()
    for a in range(4):
        heads[a * TOK:(a + 1) * TOK] = q_ref[tick, :, a * HD:(a + 1) * HD]
    own = jnp.zeros((TOK, 256), F32)
    far = jnp.zeros((TOK, 256), F32)
    for c in range(CHUNKS):
        copies[c].wait()
        if tick == 0:
            for block in range(c * 16 // CHUNKS, (c + 1) * 16 // CHUNKS):
                deep = pl.ds(block * 256, 256)
                own += dot(g_ref[block], wo_own_ref[deep])
                far += dot(g_ref[block], wo_far_ref[deep])
        else:
            deep = pl.ds(c * DEEP, DEEP)
            part = g_ref[:, :, deep].reshape(TOK, DEEP)
            own += dot(part, wo_own_ref[deep])
            far += dot(part, wo_far_ref[deep])
    keys = kv_ref[tick, :, :HD]
    values = kv_ref[tick, :, HD:]
    for a in range(4):
        side = own if a < 2 else far
        grad_heads[a * TOK:(a + 1) * TOK] = side[:, a % 2 * HD:(a % 2 + 1) * HD].astype(BF)
    grad_probs = dot_nt(grad_heads[...], values)
    attention = attention_ref[tick].reshape(4 * TOK, TOK)
    row_delta = jnp.sum(attention * grad_probs, axis=-1, keepdims=True)
    grad_scores = (attention * (grad_probs - row_delta) * SCALE).astype(BF)
    query_grad = dot(grad_scores, keys).astype(BF)
    for a in range(4):
        target = own_ref if a < 2 else far_ref
        target[:, a % 2 * HD:(a % 2 + 1) * HD] = query_grad[a * TOK:(a + 1) * TOK]
    pairs_ref[:, :HD] = dot_tn(grad_scores, heads[...]).astype(BF)
    pairs_ref[:, HD:] = dot_tn(attention.astype(BF), grad_heads[...]).astype(BF)
    for n in range(8):
        wide = pl.ds(n * 512, 512)
        out = dot_nt(own_ref[...], wq_own_ref[wide]) + dot_nt(far_ref[...], wq_far_ref[wide])
        out = out + dot_nt(pairs_ref[...], wkv_ref[wide])
        terms_ref[:, wide] = out.astype(BF)


def back(tick, grads, wo_own, wo_far, wq_own, wq_far, w_kv, queries, pairs, attention):
    return pl.pallas_call(
        functools.partial(back_kernel, tick),
        out_shape=(
            jax.ShapeDtypeStruct((TOK, WIDTH), BF),
            jax.ShapeDtypeStruct((3 * TOK, 256), BF),
        ),
        in_specs=[HBM] + [VMEM] * 8,
        out_specs=(VMEM, VMEM),
        scratch_shapes=[
            pltpu.VMEM((16, TOK, 256) if tick == 0 else (8, 16, WIDTH), BF),
            pltpu.VMEM((4 * TOK, HD), BF),
            pltpu.VMEM((4 * TOK, HD), BF),
            pltpu.SemaphoreType.DMA((CHUNKS,)),
        ],
        compiler_params=params(24),
    )(grads, wo_own, wo_far, wq_own, wq_far, w_kv, queries, pairs, attention)


def finish_kernel(first, tick, chip_ref, terms_ref, rows_ref, grad_ref, out_ref, blocks_ref, kept):
    x_at = TOK + 16 * tick
    here = pl.ds(pl.multiple_of(chip_ref[0] * 16, 16), 16)
    squares = jnp.zeros((16, 256), F32)
    products = jnp.zeros((16, 256), F32)
    for j in range(16):
        wide = pl.ds(j * 256, 256)
        x = rows_ref[j, x_at:x_at + 16].astype(F32)
        total = terms_ref[0, :, wide].astype(F32)
        for m in range(1, 8):
            total += terms_ref[m, :, wide].astype(F32)
        kept[:, wide] = total
        squares += x * x
        products += total * x
    inverse = lax.rsqrt(jnp.sum(squares, axis=-1, keepdims=True) / WIDTH + 1e-06)
    shift = jnp.sum(products, axis=-1, keepdims=True) * inverse * inverse / WIDTH
    for j in range(16):
        wide = pl.ds(j * 256, 256)
        x = rows_ref[j, x_at:x_at + 16].astype(F32)
        before = rows_ref[j, here] if first else grad_ref[:, wide]
        out = before.astype(F32) + inverse * (kept[:, wide] - x * shift)
        out = out.astype(BF)
        out_ref[:, wide] = out
        blocks_ref[j] = out


def finish(tick, chip, terms, rows, grad_rows):
    first = tick == 0
    operands = (chip.reshape(1), terms, rows) + (() if first else (grad_rows,))

    def kernel(*refs):
        if first:
            finish_kernel(first, tick, *refs[:3], None, *refs[3:])
        else:
            finish_kernel(first, tick, *refs)

    return pl.pallas_call(
        kernel,
        out_shape=(
            jax.ShapeDtypeStruct((16, WIDTH), BF),
            jax.ShapeDtypeStruct((16, 16, 256), BF),
        ),
        in_specs=[pl.BlockSpec(memory_space=pltpu.SMEM)] + [VMEM] * (len(operands) - 1),
        out_specs=(VMEM, VMEM),
        scratch_shapes=[pltpu.VMEM((16, WIDTH), F32)],
        compiler_params=params(16),
    )(*operands)


def rows_kernel(half_ref, chip_ref, rows_ref, sent_ref, held_ref):
    rows = 32
    squares = jnp.zeros((rows, 256), F32)
    for j in range(16):
        x = rows_ref[j, TOK:].astype(F32)
        squares += x * x
    inverse = lax.rsqrt(jnp.sum(squares, axis=-1, keepdims=True) / WIDTH + 1e-06)
    half = half_ref[0]
    here = pl.ds(pl.multiple_of(chip_ref[0] * 16, 16), 16)
    for j in range(8):
        wide = pl.ds(j * 256, 256)
        near, far = half * 8 + j, (1 - half) * 8 + j
        held_ref[:rows, wide] = (rows_ref[near, TOK:].astype(F32) * inverse).astype(BF)
        sent_ref[:rows, wide] = (rows_ref[far, TOK:].astype(F32) * inverse).astype(BF)
        sent_ref[rows:, wide] = rows_ref[far, here]
        held_ref[rows:, wide] = rows_ref[near, here]


def split_rows(half, chip, rows):
    return pl.pallas_call(
        rows_kernel,
        out_shape=(
            jax.ShapeDtypeStruct((48, HALF), BF),
            jax.ShapeDtypeStruct((48, HALF), BF),
        ),
        in_specs=[pl.BlockSpec(memory_space=pltpu.SMEM)] * 2 + [VMEM],
        out_specs=(VMEM, VMEM),
        compiler_params=params(16),
    )(half.reshape(1), chip.reshape(1), rows)


def fill_right(core_ref, right_ref, near, far):
    core = core_ref[0]
    for side, sources in enumerate((near, far)):
        direction = core if side == 0 else 1 - core
        for m in range(8):
            for group, source in enumerate(sources):
                at = (2 * m + direction) * 16 * len(sources) + group * 16
                value = source(m * 16)
                right_ref[pl.ds(pl.multiple_of(at, 16), 16)] = value


def columns_kernel(
    core_ref, x_hbm, after_hbm,
    near_0, near_1, near_m0, near_m1, far_0, far_1, far_m0, far_m1,
    query_ref, pairs_ref, x_ref, right_ref, sems,
):
    copies = [
        pltpu.make_async_copy(x_hbm.at[:, :32], x_ref.at[:, :32], sems.at[0]),
        pltpu.make_async_copy(x_hbm.at[:, 48:80], x_ref.at[:, 32:], sems.at[1]),
    ]
    for copy in copies:
        copy.start()

    def both_columns(ref):
        return lambda at: jnp.concatenate([ref[at:at + 16], ref[TOK + at:TOK + at + 16]], -1)

    near = [both_columns(ref) for ref in (near_0, near_1, near_m0, near_m1)]
    far = [both_columns(ref) for ref in (far_0, far_1, far_m0, far_m1)]
    fill_right(core_ref, right_ref, near, far)
    for copy in copies:
        copy.wait()
    core = core_ref[0]
    for n in range(4):
        wide = pl.ds(pl.multiple_of(core * 1024 + n * 256, 256), 256)
        both = dot_tn(x_ref[:, :, wide].reshape(1024, 256), right_ref[...])
        query_ref[wide] = both[:, :256].astype(BF)
        pairs_ref[n * 256:(n + 1) * 256] = both[:, 256:].astype(BF)
    for n in range(4):
        wide = pl.ds(pl.multiple_of((1 - core) * 1024 + n * 256, 256), 256)
        query_ref[wide] = dot_tn(x_ref[:, :, wide].reshape(1024, 256), right_ref[:, :256]).astype(BF)


def columns(core, x, after, rights):
    return pl.pallas_call(
        columns_kernel,
        out_shape=(
            jax.ShapeDtypeStruct((HALF, 256), BF),
            jax.ShapeDtypeStruct((1024, 256), BF),
        ),
        in_specs=[pl.BlockSpec(memory_space=pltpu.SMEM)] + [HBM] * 2 + [VMEM] * 8,
        out_specs=(VMEM, VMEM),
        scratch_shapes=[
            pltpu.VMEM((16, 64, HALF), BF),
            pltpu.VMEM((1024, 512), BF),
            pltpu.SemaphoreType.DMA((2,)),
        ],
        cost_estimate=pl.CostEstimate(flops=1000, bytes_accessed=1000, transcendentals=0),
        compiler_params=params(58),
    )(core.reshape(1), x, after, *rights)


def output_kernel(
    core_ref, x_hbm, near_hbm, far_hbm,
    near_0, near_m0, near_1, near_m1, far_0, far_m0, far_1, far_m1,
    out_ref, g_ref, right_ref, second_ref, second_right, sems,
):
    copies = [
        pltpu.make_async_copy(x_hbm.at[:, 32:48], g_ref.at[:, :16], sems.at[0]),
        pltpu.make_async_copy(x_hbm.at[:, 80:], g_ref.at[:, 16:], sems.at[1]),
        pltpu.make_async_copy(near_hbm, second_ref.at[:2 * TOK], sems.at[2]),
        pltpu.make_async_copy(far_hbm, second_ref.at[2 * TOK:], sems.at[3]),
    ]
    for copy in copies:
        copy.start()

    def rows(ref):
        return lambda at: ref[at:at + 16]

    fill_right(core_ref, right_ref, [rows(near_0), rows(near_m0)], [rows(far_0), rows(far_m0)])
    for n, ref in enumerate((near_1, near_m1, far_1, far_m1)):
        second_right[n * TOK:(n + 1) * TOK] = ref[...]
    for copy in copies:
        copy.wait()
    for j in range(8):
        wide = pl.ds(j * 256, 256)
        out = dot_tn(g_ref[:, :, wide].reshape(512, 256), right_ref[...])
        out += dot_tn(second_ref[:, wide], second_right[...])
        out_ref[wide] = out.astype(BF)


def output_columns(core, x, near, far, attended):
    return pl.pallas_call(
        output_kernel,
        out_shape=jax.ShapeDtypeStruct((HALF, 256), BF),
        in_specs=[pl.BlockSpec(memory_space=pltpu.SMEM)] + [HBM] * 3 + [VMEM] * 8,
        out_specs=VMEM,
        scratch_shapes=[
            pltpu.VMEM((16, 32, HALF), BF),
            pltpu.VMEM((512, 256), BF),
            pltpu.VMEM((512, HALF), BF),
            pltpu.VMEM((512, 256), BF),
            pltpu.SemaphoreType.DMA((4,)),
        ],
        cost_estimate=pl.CostEstimate(flops=1000, bytes_accessed=1000, transcendentals=0),
        compiler_params=params(58),
    )(core.reshape(1), x, near, far, *attended)


def on_device(weight_q, weight_kv, weight_o, section_inputs, saved_q, saved_kv, out_grads):
    position = lax.axis_index("section")
    column = lax.axis_index("tensor")
    core = column % 2
    z_low = column // 2 % 2
    half = (position >= 8).astype(jnp.int32)
    next_half = (position + 2 * core - 1 >= 8).astype(jnp.int32)
    w_q, w_kv, w_o = weight_q[0], weight_kv[0], weight_o[0]
    inputs = section_inputs[:, :, 0]
    grads = out_grads[:, 0]

    def pick(x, index):
        return lax.dynamic_index_in_dim(x, index, 0, keepdims=False)

    def features_of(x, which):
        return lax.dynamic_slice_in_dim(x, which * HALF, HALF, x.ndim - 1)

    by_chip = (8, 2, TOK, 256)
    tokens = inputs.reshape(2, TICKS, 8, 16, 256).transpose(2, 0, 1, 3, 4).reshape(8, 2, 32, 256)
    mixed = jnp.concatenate([jnp.broadcast_to(grads[None], by_chip), tokens], 2)
    rows = exchange16(mixed.reshape(16, TOK + 32, 256))

    wo_far = swap_core(w_o)
    queries = saved_q[:, :, 0]
    queries = jnp.concatenate([pick(queries, core), swap_core(pick(queries, 1 - core))], -1)
    wq_far = swap_core(w_q)
    pairs = pick(saved_kv[:, :, 0], core)
    attention, attended = attend(queries, pairs)
    chip = (column // 2).astype(jnp.int32)
    sent, held = split_rows(half, chip, rows)
    att_m = mirror(attended)
    near_o, near_q, near_kv = swap_core(wo_far), swap_core(wq_far), swap_core(w_kv)
    rows, sent, held, wo_far, wq_far, near_o, near_q, near_kv, attention = together(
        rows, sent, held, wo_far, wq_far, near_o, near_q, near_kv, attention
    )

    def both_chips(p):
        return (p.astype(F32) + swap_z(p).astype(F32)).astype(BF)

    def block(x, at):
        return x[at * TOK:(at + 1) * TOK]

    def held_near(x):
        return pltpu.with_memory_space_constraint(x, pltpu.VMEM)

    w_o, wo_far, w_q, wq_far, w_kv = map(held_near, (near_o, wo_far, near_q, wq_far, near_kv))

    terms, parts_0 = back(
        0, rows, w_o, wo_far, w_q, wq_far, w_kv, queries, pairs, attention
    )
    parts_0, sent = together(parts_0, sent)
    terms, att_m = together(terms, att_m)
    terms_0 = exchange8(terms.reshape(8, 16, WIDTH))
    got = mirror(sent)
    x_rows = jnp.concatenate([held, got], 0)
    terms_0, x_rows = together(terms_0, x_rows)

    grad_in_0, blocks_0 = finish(0, chip, terms_0, rows, None)
    grad_rows = next_section(grad_in_0)
    sum_0 = both_chips(block(parts_0, 2))
    grad_half = next_mirror(
        lax.dynamic_slice_in_dim(grad_in_0, (1 - next_half) * HALF, HALF, 1)
    )

    spread_1 = jnp.concatenate([grad_rows, grad_half], 1)
    spread_1 = jnp.broadcast_to(spread_1[None], (8,) + spread_1.shape)
    spread_1, parts_0, sum_0, x_rows = together(spread_1, parts_0, sum_0, x_rows)
    full_1 = exchange8(spread_1)
    x_all = gather16(x_rows)
    terms, parts_1 = back(
        1, full_1, w_o, wo_far, w_q, wq_far, w_kv, queries, pairs, attention
    )
    sum_1 = both_chips(block(parts_1, 2))
    terms, sum_1 = together(terms, sum_1)
    terms_1 = exchange8(terms.reshape(8, 16, WIDTH))
    here = jnp.stack(
        [jnp.concatenate([parts_0[:2 * TOK], sum_0], 0), jnp.concatenate([parts_1[:2 * TOK], sum_1], 0)]
    )
    late_m = mirror(here)

    att_far = swap_core(jnp.stack([attended[..., 256:], att_m[..., 256:]]))
    g_near = jnp.concatenate(
        [lax.dynamic_slice_in_dim(full_1, half * HALF, HALF, 2), full_1[:, :, WIDTH:]], 0
    ).reshape(256, HALF)
    g_far = swap_core(g_near)
    terms_1, x_all, g_far = together(terms_1, x_all, g_far)

    after, blocks_1 = finish(1, chip, terms_1, rows, grad_rows)
    out = exchange16(jnp.concatenate([blocks_0, blocks_1], 1))
    after, x_all, late_m = together(after, x_all, late_m)
    both = jnp.stack([here, late_m])
    near = jnp.concatenate([both[:, :, :TOK], both[:, :, 2 * TOK:]], 2)
    far = swap_core(both[:, :, TOK:])
    x_all = x_all.reshape(16, 96, HALF)
    grad_query, acc_kv = columns(
        core, x_all, after,
        [near[0, 0], near[0, 1], near[1, 0], near[1, 1], far[0, 0], far[0, 1], far[1, 0], far[1, 1]],
    )
    att, att_got = attended[..., :256], att_m[..., :256]
    grad_output = output_columns(
        core, x_all, g_near, g_far,
        [att[0], att_got[0], att[1], att_got[1],
         att_far[0, 0], att_far[1, 0], att_far[0, 1], att_far[1, 1]],
    )
    kept = lax.dynamic_slice_in_dim(acc_kv, half * 512, 512, 0)
    given = lax.dynamic_slice_in_dim(acc_kv, (1 - half) * 512, 512, 0)
    taken = send(given, lambda s, c: (15 - s, c) if c // 2 % 2 == s // 8 else None)
    grad_kv = jnp.where(z_low == half, kept, taken)

    input_grads = out.reshape(8, 2, TICKS, 16, 256).transpose(1, 2, 0, 3, 4)
    input_grads = input_grads.reshape(2, TICKS, 1, TOK, 256)
    return (input_grads, grad_query[None], grad_kv[None], grad_output[None])


def solution(mesh):
    placed = (
        P("section", None, "tensor"),
        P("section", None, "tensor"),
        P("section", None, "tensor"),
        P(None, None, "section", None, "tensor"),
        P(None, None, "section", None, "tensor"),
        P(None, None, "section", None, "tensor"),
        P(None, "section", None, "tensor"),
    )
    return jax.shard_map(
        on_device,
        mesh=mesh,
        in_specs=placed,
        out_specs=(
            P(None, None, "section", None, "tensor"),
            P("section", None, "tensor"),
            P("section", None, "tensor"),
            P("section", None, "tensor"),
        ),
        check_vma=False,
    )
```

```python
import functools

import jax
import jax.numpy as jnp
from jax import lax
from jax.experimental import pallas as pl
from jax.experimental.pallas import tpu as pltpu
from jax.sharding import PartitionSpec as P

HD = 128
TICKS = 2
TOK = 128
WIDTH = 4096
HALF = WIDTH // 2
SCALE = HD ** (-0.5)
BF = jnp.bfloat16
F32 = jnp.float32

SAME_CORE = [[core + 2 * chip for chip in range(8)] for core in range(2)]
VMEM = pl.BlockSpec(memory_space=pltpu.VMEM)
HBM = pl.BlockSpec(memory_space=pl.ANY)


def send(x, route):
    pairs = []
    for section in range(16):
        for tensor in range(16):
            target = route(section, tensor)
            if target is not None:
                pairs.append((section * 16 + tensor, target[0] * 16 + target[1]))
    return lax.ppermute(x, ("section", "tensor"), pairs)


def swap_core(x):
    return lax.ppermute(x, "tensor", [(i, i ^ 1) for i in range(16)])


def swap_z(x):
    return lax.ppermute(x, "tensor", [(i, i ^ 2) for i in range(16)])


def swap_y(x, k):
    return lax.ppermute(x, "tensor", [(i, i ^ 4 * k) for i in range(16)])


def mirror(x):
    return lax.ppermute(x, "section", [(i, 15 - i) for i in range(16)])


def next_section(x):
    def route(s, c):
        target = s - 1 if c % 2 == 0 else s + 1
        return (target, c) if 0 <= target < 16 else None

    return send(x, route)


def next_mirror(x):
    def route(s, c):
        target = s - 1 if c % 2 == 0 else s + 1
        return (15 - target, c) if 0 <= target < 16 else None

    return send(x, route)


def exchange8(x):
    return lax.all_to_all(x, "tensor", 0, 0, axis_index_groups=SAME_CORE, tiled=True)


def exchange16(x):
    return lax.all_to_all(x, "tensor", 0, 0, tiled=True)


def gather16(x):
    return lax.all_gather(x, "tensor", axis=0, tiled=True)


def dot(a, b):
    return jnp.dot(a, b, preferred_element_type=F32)


def dot_nt(a, b):
    return lax.dot_general(a, b, (((1,), (1,)), ((), ())), preferred_element_type=F32)


def dot_tn(a, b):
    return lax.dot_general(a, b, (((0,), (0,)), ((), ())), preferred_element_type=F32)


def together(*values):
    return lax.optimization_barrier(values)


def params(mib):
    return pltpu.CompilerParams(vmem_limit_bytes=mib * 2**20)


def first_kernel(grads_ref, inputs_ref, out_ref):
    for m in range(8):
        for r in range(2):
            out_ref[2 * m + r, :TOK] = grads_ref[r]
            for t in range(TICKS):
                at = TOK + 16 * t
                out_ref[2 * m + r, at:at + 16] = inputs_ref[r, t, m * 16:m * 16 + 16]


def first_blocks(grads, inputs):
    return pl.pallas_call(
        first_kernel,
        out_shape=jax.ShapeDtypeStruct((16, TOK + 32, 256), BF),
        in_specs=[VMEM] * 2,
        out_specs=VMEM,
        compiler_params=params(16),
    )(grads, inputs)


def attend_kernel(q_ref, kv_ref, attention_ref, attended_ref):
    rows = lax.broadcasted_iota(jnp.int32, (TOK, TOK), 0)
    columns = lax.broadcasted_iota(jnp.int32, (TOK, TOK), 1)
    causal = rows >= columns
    for t in range(TICKS):
        keys = kv_ref[t, :, :HD]
        values = kv_ref[t, :, HD:]
        for a in range(4):
            head = slice(a * HD, (a + 1) * HD)
            scores = jnp.where(causal, dot_nt(q_ref[t, :, head], keys) * SCALE, -1e30)
            weights = jnp.exp(scores - jnp.max(scores, axis=-1, keepdims=True))
            weights = weights / jnp.sum(weights, axis=-1, keepdims=True)
            attention_ref[t, a] = weights
            attended_ref[t, :, head] = dot(weights.astype(BF), values).astype(BF)


def attend(queries, pairs):
    return pl.pallas_call(
        attend_kernel,
        out_shape=(
            jax.ShapeDtypeStruct((TICKS, 4, TOK, TOK), F32),
            jax.ShapeDtypeStruct((TICKS, TOK, 4 * HD), BF),
        ),
        in_specs=[VMEM] * 2,
        out_specs=(VMEM, VMEM),
        compiler_params=params(16),
    )(queries, pairs)


CHUNKS = 4
DEEP = WIDTH // CHUNKS


def back_kernel(
    tick,
    g_hbm, wo_own_ref, wo_far_ref, wq_own_ref, wq_far_ref, wkv_ref, q_ref, kv_ref, attention_ref,
    terms_ref, parts_ref,
    g_ref, grad_heads, heads, g_sems,
):
    own_ref, far_ref, pairs_ref = (parts_ref.at[pl.ds(n * TOK, TOK)] for n in range(3))
    copies = []
    for c in range(CHUNKS):
        if tick == 0:
            part = pl.ds(c * 16 // CHUNKS, 16 // CHUNKS)
            copies.append(pltpu.make_async_copy(g_hbm.at[part, :TOK], g_ref.at[part], g_sems.at[c]))
        else:
            deep = pl.ds(c * DEEP, DEEP)
            copies.append(pltpu.make_async_copy(g_hbm.at[:, :, deep], g_ref.at[:, :, deep], g_sems.at[c]))
    for copy in copies:
        copy.start()
    for a in range(4):
        heads[a * TOK:(a + 1) * TOK] = q_ref[tick, :, a * HD:(a + 1) * HD]
    own = jnp.zeros((TOK, 256), F32)
    far = jnp.zeros((TOK, 256), F32)
    for c in range(CHUNKS):
        copies[c].wait()
        if tick == 0:
            for block in range(c * 16 // CHUNKS, (c + 1) * 16 // CHUNKS):
                deep = pl.ds(block * 256, 256)
                own += dot(g_ref[block], wo_own_ref[deep])
                far += dot(g_ref[block], wo_far_ref[deep])
        else:
            deep = pl.ds(c * DEEP, DEEP)
            part = g_ref[:, :, deep].reshape(TOK, DEEP)
            own += dot(part, wo_own_ref[deep])
            far += dot(part, wo_far_ref[deep])
    keys = kv_ref[tick, :, :HD]
    values = kv_ref[tick, :, HD:]
    for a in range(4):
        side = own if a < 2 else far
        grad_heads[a * TOK:(a + 1) * TOK] = side[:, a % 2 * HD:(a % 2 + 1) * HD].astype(BF)
    grad_probs = dot_nt(grad_heads[...], values)
    attention = attention_ref[tick].reshape(4 * TOK, TOK)
    row_delta = jnp.sum(attention * grad_probs, axis=-1, keepdims=True)
    grad_scores = (attention * (grad_probs - row_delta) * SCALE).astype(BF)
    query_grad = dot(grad_scores, keys).astype(BF)
    for a in range(4):
        target = own_ref if a < 2 else far_ref
        target[:, a % 2 * HD:(a % 2 + 1) * HD] = query_grad[a * TOK:(a + 1) * TOK]
    pairs_ref[:, :HD] = dot_tn(grad_scores, heads[...]).astype(BF)
    pairs_ref[:, HD:] = dot_tn(attention.astype(BF), grad_heads[...]).astype(BF)
    for n in range(8):
        wide = pl.ds(n * 512, 512)
        out = dot_nt(own_ref[...], wq_own_ref[wide]) + dot_nt(far_ref[...], wq_far_ref[wide])
        out = out + dot_nt(pairs_ref[...], wkv_ref[wide])
        terms_ref[:, wide] = out.astype(BF)


def back(tick, grads, wo_own, wo_far, wq_own, wq_far, w_kv, queries, pairs, attention):
    return pl.pallas_call(
        functools.partial(back_kernel, tick),
        out_shape=(
            jax.ShapeDtypeStruct((TOK, WIDTH), BF),
            jax.ShapeDtypeStruct((3 * TOK, 256), BF),
        ),
        in_specs=[HBM] + [VMEM] * 8,
        out_specs=(VMEM, VMEM),
        scratch_shapes=[
            pltpu.VMEM((16, TOK, 256) if tick == 0 else (8, 16, WIDTH), BF),
            pltpu.VMEM((4 * TOK, HD), BF),
            pltpu.VMEM((4 * TOK, HD), BF),
            pltpu.SemaphoreType.DMA((CHUNKS,)),
        ],
        compiler_params=params(24),
    )(grads, wo_own, wo_far, wq_own, wq_far, w_kv, queries, pairs, attention)


def finish_kernel(first, tick, chip_ref, terms_ref, rows_ref, grad_ref, before_ref, out_ref, blocks_ref, kept):
    x_at = TOK + 16 * tick
    here = pl.ds(pl.multiple_of(chip_ref[0] * 16, 16), 16)
    squares = jnp.zeros((16, 256), F32)
    products = jnp.zeros((16, 256), F32)
    for j in range(16):
        wide = pl.ds(j * 256, 256)
        x = rows_ref[j, x_at:x_at + 16].astype(F32)
        total = terms_ref[0, :, wide].astype(F32)
        for m in range(1, 8):
            total += terms_ref[m, :, wide].astype(F32)
        kept[:, wide] = total
        squares += x * x
        products += total * x
    inverse = lax.rsqrt(jnp.sum(squares, axis=-1, keepdims=True) / WIDTH + 1e-06)
    shift = jnp.sum(products, axis=-1, keepdims=True) * inverse * inverse / WIDTH
    for j in range(16):
        wide = pl.ds(j * 256, 256)
        x = rows_ref[j, x_at:x_at + 16].astype(F32)
        before = rows_ref[j, here] if first else grad_ref[:, wide]
        out = before.astype(F32) + inverse * (kept[:, wide] - x * shift)
        out = out.astype(BF)
        out_ref[:, wide] = out
        if first:
            blocks_ref[j] = out
        else:
            blocks_ref[j, :16] = before_ref[j]
            blocks_ref[j, 16:] = out


def finish(tick, chip, terms, rows, grad_rows=None, blocks=None):
    first = tick == 0
    operands = (chip.reshape(1), terms, rows) + (() if first else (grad_rows, blocks))

    def kernel(*refs):
        if first:
            finish_kernel(first, tick, *refs[:3], None, None, *refs[3:])
        else:
            finish_kernel(first, tick, *refs)

    return pl.pallas_call(
        kernel,
        out_shape=(
            jax.ShapeDtypeStruct((16, WIDTH), BF),
            jax.ShapeDtypeStruct((16, 16 if first else 32, 256), BF),
        ),
        in_specs=[pl.BlockSpec(memory_space=pltpu.SMEM)] + [VMEM] * (len(operands) - 1),
        out_specs=(VMEM, VMEM),
        scratch_shapes=[pltpu.VMEM((16, WIDTH), F32)],
        compiler_params=params(16),
    )(*operands)


def rows_kernel(half_ref, chip_ref, rows_ref, sent_ref, held_ref):
    rows = 32
    squares = jnp.zeros((rows, 256), F32)
    for j in range(16):
        x = rows_ref[j, TOK:].astype(F32)
        squares += x * x
    inverse = lax.rsqrt(jnp.sum(squares, axis=-1, keepdims=True) / WIDTH + 1e-06)
    half = half_ref[0]
    here = pl.ds(pl.multiple_of(chip_ref[0] * 16, 16), 16)
    for j in range(8):
        wide = pl.ds(j * 256, 256)
        near, far = half * 8 + j, (1 - half) * 8 + j
        held_ref[:rows, wide] = (rows_ref[near, TOK:].astype(F32) * inverse).astype(BF)
        sent_ref[:rows, wide] = (rows_ref[far, TOK:].astype(F32) * inverse).astype(BF)
        sent_ref[rows:, wide] = rows_ref[far, here]
        held_ref[rows:, wide] = rows_ref[near, here]


def split_rows(half, chip, rows):
    return pl.pallas_call(
        rows_kernel,
        out_shape=(
            jax.ShapeDtypeStruct((48, HALF), BF),
            jax.ShapeDtypeStruct((48, HALF), BF),
        ),
        in_specs=[pl.BlockSpec(memory_space=pltpu.SMEM)] * 2 + [VMEM],
        out_specs=(VMEM, VMEM),
        compiler_params=params(16),
    )(half.reshape(1), chip.reshape(1), rows)


def fill_right(core_ref, right_ref, near, far):
    core = core_ref[0]
    for side, sources in enumerate((near, far)):
        direction = core if side == 0 else 1 - core
        for m in range(8):
            for group, source in enumerate(sources):
                at = (2 * m + direction) * 16 * len(sources) + group * 16
                value = source(m * 16)
                right_ref[pl.ds(pl.multiple_of(at, 16), 16)] = value


def columns_kernel(
    core_ref, x_hbm, after_hbm, here_ref, got_ref, far_ref, far_got_ref,
    query_ref, pairs_ref, x_ref, right_ref, sems,
):
    copies = [
        pltpu.make_async_copy(x_hbm.at[:, :32], x_ref.at[:, :32], sems.at[0]),
        pltpu.make_async_copy(x_hbm.at[:, 48:80], x_ref.at[:, 32:], sems.at[1]),
    ]
    for copy in copies:
        copy.start()

    def both_columns(ref, t, pairs_at):
        return lambda at: jnp.concatenate(
            [ref[t, at:at + 16], ref[t, pairs_at + at:pairs_at + at + 16]], -1
        )

    near = [both_columns(ref, t, 2 * TOK) for ref in (here_ref, got_ref) for t in range(TICKS)]
    far = [both_columns(ref, t, TOK) for ref in (far_ref, far_got_ref) for t in range(TICKS)]
    fill_right(core_ref, right_ref, near, far)
    for copy in copies:
        copy.wait()
    core = core_ref[0]
    for n in range(4):
        wide = pl.ds(pl.multiple_of(core * 1024 + n * 256, 256), 256)
        both = dot_tn(x_ref[:, :, wide].reshape(1024, 256), right_ref[...])
        query_ref[wide] = both[:, :256].astype(BF)
        pairs_ref[n * 256:(n + 1) * 256] = both[:, 256:].astype(BF)
    for n in range(4):
        wide = pl.ds(pl.multiple_of((1 - core) * 1024 + n * 256, 256), 256)
        query_ref[wide] = dot_tn(x_ref[:, :, wide].reshape(1024, 256), right_ref[:, :256]).astype(BF)


def columns(core, x, after, rights):
    return pl.pallas_call(
        columns_kernel,
        out_shape=(
            jax.ShapeDtypeStruct((HALF, 256), BF),
            jax.ShapeDtypeStruct((1024, 256), BF),
        ),
        in_specs=[pl.BlockSpec(memory_space=pltpu.SMEM)] + [HBM] * 2 + [VMEM] * 4,
        out_specs=(VMEM, VMEM),
        scratch_shapes=[
            pltpu.VMEM((16, 64, HALF), BF),
            pltpu.VMEM((1024, 512), BF),
            pltpu.SemaphoreType.DMA((2,)),
        ],
        cost_estimate=pl.CostEstimate(flops=1000, bytes_accessed=1000, transcendentals=0),
        compiler_params=params(58),
    )(core.reshape(1), x, after, *rights)


def output_kernel(
    core_ref, x_hbm, near_hbm, far_hbm, here, got, far,
    out_ref, g_ref, right_ref, second_ref, second_right, sems,
):
    copies = [
        pltpu.make_async_copy(x_hbm.at[:, 32:48], g_ref.at[:, :16], sems.at[0]),
        pltpu.make_async_copy(x_hbm.at[:, 80:], g_ref.at[:, 16:], sems.at[1]),
        pltpu.make_async_copy(near_hbm, second_ref.at[:2 * TOK], sems.at[2]),
        pltpu.make_async_copy(far_hbm, second_ref.at[2 * TOK:], sems.at[3]),
    ]
    for copy in copies:
        copy.start()

    near_rows = [lambda at, ref=ref: ref[0, at:at + 16, :256] for ref in (here, got)]
    far_rows = [lambda at, s=s: far[s, 0, at:at + 16] for s in range(2)]
    fill_right(core_ref, right_ref, near_rows, far_rows)
    for n, ref in enumerate((here, got)):
        second_right[n * TOK:(n + 1) * TOK] = ref[1, :, :256]
    for s in range(2):
        second_right[(2 + s) * TOK:(3 + s) * TOK] = far[s, 1]
    for copy in copies:
        copy.wait()
    for j in range(8):
        wide = pl.ds(j * 256, 256)
        out = dot_tn(g_ref[:, :, wide].reshape(512, 256), right_ref[...])
        out += dot_tn(second_ref[:, wide], second_right[...])
        out_ref[wide] = out.astype(BF)


def output_columns(core, x, near, far, attended):
    return pl.pallas_call(
        output_kernel,
        out_shape=jax.ShapeDtypeStruct((HALF, 256), BF),
        in_specs=[pl.BlockSpec(memory_space=pltpu.SMEM)] + [HBM] * 3 + [VMEM] * 3,
        out_specs=VMEM,
        scratch_shapes=[
            pltpu.VMEM((16, 32, HALF), BF),
            pltpu.VMEM((512, 256), BF),
            pltpu.VMEM((512, HALF), BF),
            pltpu.VMEM((512, 256), BF),
            pltpu.SemaphoreType.DMA((4,)),
        ],
        cost_estimate=pl.CostEstimate(flops=1000, bytes_accessed=1000, transcendentals=0),
        compiler_params=params(58),
    )(core.reshape(1), x, near, far, *attended)


def on_device(weight_q, weight_kv, weight_o, section_inputs, saved_q, saved_kv, out_grads):
    position = lax.axis_index("section")
    column = lax.axis_index("tensor")
    core = column % 2
    z_low = column // 2 % 2
    half = (position >= 8).astype(jnp.int32)
    next_half = (position + 2 * core - 1 >= 8).astype(jnp.int32)
    w_q, w_kv, w_o = weight_q[0], weight_kv[0], weight_o[0]
    inputs = section_inputs[:, :, 0]
    grads = out_grads[:, 0]

    def pick(x, index):
        return lax.dynamic_index_in_dim(x, index, 0, keepdims=False)

    def features_of(x, which):
        return lax.dynamic_slice_in_dim(x, which * HALF, HALF, x.ndim - 1)

    rows = exchange16(first_blocks(grads, inputs))

    wo_far = swap_core(w_o)
    queries = saved_q[:, :, 0]
    queries = jnp.concatenate([pick(queries, core), swap_core(pick(queries, 1 - core))], -1)
    wq_far = swap_core(w_q)
    pairs = pick(saved_kv[:, :, 0], core)
    attention, attended = attend(queries, pairs)
    chip = (column // 2).astype(jnp.int32)
    sent, held = split_rows(half, chip, rows)
    att_m = mirror(attended)
    near_o, near_q, near_kv = swap_core(wo_far), swap_core(wq_far), swap_core(w_kv)
    rows, sent, held, wo_far, wq_far, near_o, near_q, near_kv, attention = together(
        rows, sent, held, wo_far, wq_far, near_o, near_q, near_kv, attention
    )

    def both_chips(p):
        return (p.astype(F32) + swap_z(p).astype(F32)).astype(BF)

    def block(x, at):
        return x[at * TOK:(at + 1) * TOK]

    def held_near(x):
        return pltpu.with_memory_space_constraint(x, pltpu.VMEM)

    w_o, wo_far, w_q, wq_far, w_kv = map(held_near, (near_o, wo_far, near_q, wq_far, near_kv))

    terms, parts_0 = back(
        0, rows, w_o, wo_far, w_q, wq_far, w_kv, queries, pairs, attention
    )
    parts_0, sent = together(parts_0, sent)
    terms, att_m = together(terms, att_m)
    terms_0 = exchange8(terms.reshape(8, 16, WIDTH))
    got = mirror(sent)
    terms_0, got = together(terms_0, got)

    grad_in_0, blocks_0 = finish(0, chip, terms_0, rows)
    grad_rows = next_section(grad_in_0)
    sum_0 = both_chips(block(parts_0, 2))
    grad_half = next_mirror(
        lax.dynamic_slice_in_dim(grad_in_0, (1 - next_half) * HALF, HALF, 1)
    )

    spread_1 = jnp.concatenate([grad_rows, grad_half], 1)
    spread_1 = jnp.broadcast_to(spread_1[None], (8,) + spread_1.shape)
    x_rows = jnp.concatenate([held, got], 0)
    spread_1, parts_0, sum_0, x_rows = together(spread_1, parts_0, sum_0, x_rows)
    full_1 = exchange8(spread_1)
    x_all = gather16(x_rows)
    terms, parts_1 = back(
        1, full_1, w_o, wo_far, w_q, wq_far, w_kv, queries, pairs, attention
    )
    sum_1 = both_chips(block(parts_1, 2))
    terms, sum_1 = together(terms, sum_1)
    terms_1 = exchange8(terms.reshape(8, 16, WIDTH))
    here = jnp.stack(
        [jnp.concatenate([parts_0[:2 * TOK], sum_0], 0), jnp.concatenate([parts_1[:2 * TOK], sum_1], 0)]
    )
    late_m = mirror(here)
    far_here = swap_core(here[:, TOK:])

    att_far = swap_core(jnp.stack([attended[..., 256:], att_m[..., 256:]]))
    g_near = jnp.concatenate(
        [lax.dynamic_slice_in_dim(full_1, half * HALF, HALF, 2), full_1[:, :, WIDTH:]], 0
    ).reshape(256, HALF)
    g_far = swap_core(g_near)
    terms_1, x_all, g_far = together(terms_1, x_all, g_far)

    after, blocks_1 = finish(1, chip, terms_1, rows, grad_rows, blocks_0)
    out = exchange16(blocks_1)
    after, x_all, late_m = together(after, x_all, late_m)
    far_late = swap_core(late_m[:, TOK:])
    x_all = x_all.reshape(16, 96, HALF)
    grad_query, acc_kv = columns(core, x_all, after, [here, late_m, far_here, far_late])
    grad_output = output_columns(core, x_all, g_near, g_far, [attended, att_m, att_far])
    kept = lax.dynamic_slice_in_dim(acc_kv, half * 512, 512, 0)
    given = lax.dynamic_slice_in_dim(acc_kv, (1 - half) * 512, 512, 0)
    taken = send(given, lambda s, c: (15 - s, c) if c // 2 % 2 == s // 8 else None)
    grad_kv = jnp.where(z_low == half, kept, taken)

    input_grads = out.reshape(8, 2, TICKS, 16, 256).transpose(1, 2, 0, 3, 4)
    input_grads = input_grads.reshape(2, TICKS, 1, TOK, 256)
    return (input_grads, grad_query[None], grad_kv[None], grad_output[None])


def solution(mesh):
    placed = (
        P("section", None, "tensor"),
        P("section", None, "tensor"),
        P("section", None, "tensor"),
        P(None, None, "section", None, "tensor"),
        P(None, None, "section", None, "tensor"),
        P(None, None, "section", None, "tensor"),
        P(None, "section", None, "tensor"),
    )
    return jax.shard_map(
        on_device,
        mesh=mesh,
        in_specs=placed,
        out_specs=(
            P(None, None, "section", None, "tensor"),
            P("section", None, "tensor"),
            P("section", None, "tensor"),
            P("section", None, "tensor"),
        ),
        check_vma=False,
    )
```

```python
import functools

import jax
import jax.numpy as jnp
from jax import lax
from jax.experimental import pallas as pl
from jax.experimental.pallas import tpu as pltpu
from jax.sharding import PartitionSpec as P

HD = 128
TICKS = 2
TOK = 128
WIDTH = 4096
HALF = WIDTH // 2
SCALE = HD ** (-0.5)
BF = jnp.bfloat16
F32 = jnp.float32

SAME_CORE = [[core + 2 * chip for chip in range(8)] for core in range(2)]
VMEM = pl.BlockSpec(memory_space=pltpu.VMEM)
HBM = pl.BlockSpec(memory_space=pl.ANY)


def send(x, route):
    pairs = []
    for section in range(16):
        for tensor in range(16):
            target = route(section, tensor)
            if target is not None:
                pairs.append((section * 16 + tensor, target[0] * 16 + target[1]))
    return lax.ppermute(x, ("section", "tensor"), pairs)


def swap_core(x):
    return lax.ppermute(x, "tensor", [(i, i ^ 1) for i in range(16)])


def swap_z(x):
    return lax.ppermute(x, "tensor", [(i, i ^ 2) for i in range(16)])


def swap_y(x, k):
    return lax.ppermute(x, "tensor", [(i, i ^ 4 * k) for i in range(16)])


def mirror(x):
    return lax.ppermute(x, "section", [(i, 15 - i) for i in range(16)])


def next_section(x):
    def route(s, c):
        target = s - 1 if c % 2 == 0 else s + 1
        return (target, c) if 0 <= target < 16 else None

    return send(x, route)


def next_mirror(x):
    def route(s, c):
        target = s - 1 if c % 2 == 0 else s + 1
        return (15 - target, c) if 0 <= target < 16 else None

    return send(x, route)


def exchange8(x):
    return lax.all_to_all(x, "tensor", 0, 0, axis_index_groups=SAME_CORE, tiled=True)


def exchange16(x):
    return lax.all_to_all(x, "tensor", 0, 0, tiled=True)


def gather16(x):
    return lax.all_gather(x, "tensor", axis=0, tiled=True)


def dot(a, b):
    return jnp.dot(a, b, preferred_element_type=F32)


def dot_nt(a, b):
    return lax.dot_general(a, b, (((1,), (1,)), ((), ())), preferred_element_type=F32)


def dot_tn(a, b):
    return lax.dot_general(a, b, (((0,), (0,)), ((), ())), preferred_element_type=F32)


def together(*values):
    return lax.optimization_barrier(values)


def params(mib):
    return pltpu.CompilerParams(vmem_limit_bytes=mib * 2**20)


def first_kernel(grads_ref, inputs_ref, out_ref):
    for m in range(8):
        for r in range(2):
            out_ref[2 * m + r, :TOK] = grads_ref[r]
            for t in range(TICKS):
                at = TOK + 16 * t
                out_ref[2 * m + r, at:at + 16] = inputs_ref[r, t, m * 16:m * 16 + 16]


def first_blocks(grads, inputs):
    return pl.pallas_call(
        first_kernel,
        out_shape=jax.ShapeDtypeStruct((16, TOK + 32, 256), BF),
        in_specs=[VMEM] * 2,
        out_specs=VMEM,
        compiler_params=params(16),
    )(grads, inputs)


def attend_kernel(q_ref, kv_ref, attention_ref, attended_ref):
    rows = lax.broadcasted_iota(jnp.int32, (TOK, TOK), 0)
    columns = lax.broadcasted_iota(jnp.int32, (TOK, TOK), 1)
    causal = rows >= columns
    for t in range(TICKS):
        keys = kv_ref[t, :, :HD]
        values = kv_ref[t, :, HD:]
        for a in range(4):
            head = slice(a * HD, (a + 1) * HD)
            scores = jnp.where(causal, dot_nt(q_ref[t, :, head], keys) * SCALE, -1e30)
            weights = jnp.exp(scores - jnp.max(scores, axis=-1, keepdims=True))
            weights = weights / jnp.sum(weights, axis=-1, keepdims=True)
            attention_ref[t, a] = weights
            attended_ref[t, :, head] = dot(weights.astype(BF), values).astype(BF)


def attend(queries, pairs):
    return pl.pallas_call(
        attend_kernel,
        out_shape=(
            jax.ShapeDtypeStruct((TICKS, 4, TOK, TOK), F32),
            jax.ShapeDtypeStruct((TICKS, TOK, 4 * HD), BF),
        ),
        in_specs=[VMEM] * 2,
        out_specs=(VMEM, VMEM),
        compiler_params=params(16),
    )(queries, pairs)


CHUNKS = 4
DEEP = WIDTH // CHUNKS


def back_kernel(
    tick,
    g_hbm, wo_own_ref, wo_far_ref, wq_own_ref, wq_far_ref, wkv_ref, q_ref, kv_ref, attention_ref,
    terms_ref, parts_ref,
    g_ref, grad_heads, heads, g_sems,
):
    own_ref, far_ref, pairs_ref = (parts_ref.at[pl.ds(n * TOK, TOK)] for n in range(3))
    copies = []
    for c in range(CHUNKS):
        if tick == 0:
            part = pl.ds(c * 16 // CHUNKS, 16 // CHUNKS)
            copies.append(pltpu.make_async_copy(g_hbm.at[part, :TOK], g_ref.at[part], g_sems.at[c]))
        else:
            deep = pl.ds(c * DEEP, DEEP)
            copies.append(pltpu.make_async_copy(g_hbm.at[:, :, deep], g_ref.at[:, :, deep], g_sems.at[c]))
    for copy in copies:
        copy.start()
    for a in range(4):
        heads[a * TOK:(a + 1) * TOK] = q_ref[tick, :, a * HD:(a + 1) * HD]
    own = jnp.zeros((TOK, 256), F32)
    far = jnp.zeros((TOK, 256), F32)
    for c in range(CHUNKS):
        copies[c].wait()
        if tick == 0:
            for block in range(c * 16 // CHUNKS, (c + 1) * 16 // CHUNKS):
                deep = pl.ds(block * 256, 256)
                own += dot(g_ref[block], wo_own_ref[deep])
                far += dot(g_ref[block], wo_far_ref[deep])
        else:
            deep = pl.ds(c * DEEP, DEEP)
            part = g_ref[:, :, deep].reshape(TOK, DEEP)
            own += dot(part, wo_own_ref[deep])
            far += dot(part, wo_far_ref[deep])
    keys = kv_ref[tick, :, :HD]
    values = kv_ref[tick, :, HD:]
    for a in range(4):
        side = own if a < 2 else far
        grad_heads[a * TOK:(a + 1) * TOK] = side[:, a % 2 * HD:(a % 2 + 1) * HD].astype(BF)
    grad_probs = dot_nt(grad_heads[...], values)
    attention = attention_ref[tick].reshape(4 * TOK, TOK)
    row_delta = jnp.sum(attention * grad_probs, axis=-1, keepdims=True)
    grad_scores = (attention * (grad_probs - row_delta) * SCALE).astype(BF)
    query_grad = dot(grad_scores, keys).astype(BF)
    for a in range(4):
        target = own_ref if a < 2 else far_ref
        target[:, a % 2 * HD:(a % 2 + 1) * HD] = query_grad[a * TOK:(a + 1) * TOK]
    pairs_ref[:, :HD] = dot_tn(grad_scores, heads[...]).astype(BF)
    pairs_ref[:, HD:] = dot_tn(attention.astype(BF), grad_heads[...]).astype(BF)
    for n in range(8):
        wide = pl.ds(n * 512, 512)
        out = dot_nt(own_ref[...], wq_own_ref[wide]) + dot_nt(far_ref[...], wq_far_ref[wide])
        out = out + dot_nt(pairs_ref[...], wkv_ref[wide])
        terms_ref[:, wide] = out.astype(BF)


def back(tick, grads, wo_own, wo_far, wq_own, wq_far, w_kv, queries, pairs, attention):
    return pl.pallas_call(
        functools.partial(back_kernel, tick),
        out_shape=(
            jax.ShapeDtypeStruct((TOK, WIDTH), BF),
            jax.ShapeDtypeStruct((3 * TOK, 256), BF),
        ),
        in_specs=[HBM] + [VMEM] * 8,
        out_specs=(VMEM, VMEM),
        scratch_shapes=[
            pltpu.VMEM((16, TOK, 256) if tick == 0 else (8, 16, WIDTH), BF),
            pltpu.VMEM((4 * TOK, HD), BF),
            pltpu.VMEM((4 * TOK, HD), BF),
            pltpu.SemaphoreType.DMA((CHUNKS,)),
        ],
        compiler_params=params(24),
    )(grads, wo_own, wo_far, wq_own, wq_far, w_kv, queries, pairs, attention)


LAST_ROWS = 64


def finish_kernel(first, tick, chip_ref, terms_ref, rows_ref, grad_ref, before_ref, out_ref, blocks_ref, kept):
    x_at = TOK + 16 * tick
    here = pl.ds(pl.multiple_of(chip_ref[0] * 16, 16), 16)
    squares = jnp.zeros((16, 256), F32)
    products = jnp.zeros((16, 256), F32)
    for j in range(16):
        wide = pl.ds(j * 256, 256)
        x = rows_ref[j, x_at:x_at + 16].astype(F32)
        total = terms_ref[0, :, wide].astype(F32)
        for m in range(1, 8):
            total += terms_ref[m, :, wide].astype(F32)
        kept[:, wide] = total
        squares += x * x
        products += total * x
    inverse = lax.rsqrt(jnp.sum(squares, axis=-1, keepdims=True) / WIDTH + 1e-06)
    shift = jnp.sum(products, axis=-1, keepdims=True) * inverse * inverse / WIDTH
    for j in range(16):
        wide = pl.ds(j * 256, 256)
        x = rows_ref[j, x_at:x_at + 16].astype(F32)
        before = rows_ref[j, here] if first else grad_ref[:, wide]
        out = before.astype(F32) + inverse * (kept[:, wide] - x * shift)
        out = out.astype(BF)
        out_ref[:, wide] = out
        if first:
            blocks_ref[j] = out
        else:
            blocks_ref[j, :16] = before_ref[j]
            for copy in range(1, blocks_ref.shape[1] // 16):
                blocks_ref[j, copy * 16:copy * 16 + 16] = out


def finish(tick, chip, terms, rows, grad_rows=None, blocks=None):
    first = tick == 0
    operands = (chip.reshape(1), terms, rows) + (() if first else (grad_rows, blocks))

    def kernel(*refs):
        if first:
            finish_kernel(first, tick, *refs[:3], None, None, *refs[3:])
        else:
            finish_kernel(first, tick, *refs)

    return pl.pallas_call(
        kernel,
        out_shape=(
            jax.ShapeDtypeStruct((16, WIDTH), BF),
            jax.ShapeDtypeStruct((16, 16 if first else LAST_ROWS, 256), BF),
        ),
        in_specs=[pl.BlockSpec(memory_space=pltpu.SMEM)] + [VMEM] * (len(operands) - 1),
        out_specs=(VMEM, VMEM),
        scratch_shapes=[pltpu.VMEM((16, WIDTH), F32)],
        compiler_params=params(16),
    )(*operands)


def rows_kernel(half_ref, chip_ref, rows_ref, sent_ref, held_ref):
    rows = 32
    squares = jnp.zeros((rows, 256), F32)
    for j in range(16):
        x = rows_ref[j, TOK:].astype(F32)
        squares += x * x
    inverse = lax.rsqrt(jnp.sum(squares, axis=-1, keepdims=True) / WIDTH + 1e-06)
    half = half_ref[0]
    here = pl.ds(pl.multiple_of(chip_ref[0] * 16, 16), 16)
    for j in range(8):
        wide = pl.ds(j * 256, 256)
        near, far = half * 8 + j, (1 - half) * 8 + j
        held_ref[:rows, wide] = (rows_ref[near, TOK:].astype(F32) * inverse).astype(BF)
        sent_ref[:rows, wide] = (rows_ref[far, TOK:].astype(F32) * inverse).astype(BF)
        sent_ref[rows:, wide] = rows_ref[far, here]
        held_ref[rows:, wide] = rows_ref[near, here]


def split_rows(half, chip, rows):
    return pl.pallas_call(
        rows_kernel,
        out_shape=(
            jax.ShapeDtypeStruct((48, HALF), BF),
            jax.ShapeDtypeStruct((48, HALF), BF),
        ),
        in_specs=[pl.BlockSpec(memory_space=pltpu.SMEM)] * 2 + [VMEM],
        out_specs=(VMEM, VMEM),
        compiler_params=params(16),
    )(half.reshape(1), chip.reshape(1), rows)


def fill_right(core_ref, right_ref, near, far):
    core = core_ref[0]
    for side, sources in enumerate((near, far)):
        direction = core if side == 0 else 1 - core
        for m in range(8):
            for group, source in enumerate(sources):
                at = (2 * m + direction) * 16 * len(sources) + group * 16
                value = source(m * 16)
                right_ref[pl.ds(pl.multiple_of(at, 16), 16)] = value


def columns_kernel(
    core_ref, x_hbm, after_hbm, here_ref, got_ref, far_ref, far_got_ref,
    query_ref, pairs_ref, x_ref, right_ref, sems,
):
    copies = [
        pltpu.make_async_copy(x_hbm.at[:, :32], x_ref.at[:, :32], sems.at[0]),
        pltpu.make_async_copy(x_hbm.at[:, 48:80], x_ref.at[:, 32:], sems.at[1]),
    ]
    for copy in copies:
        copy.start()

    def both_columns(ref, t, pairs_at):
        return lambda at: jnp.concatenate(
            [ref[t, at:at + 16], ref[t, pairs_at + at:pairs_at + at + 16]], -1
        )

    near = [both_columns(ref, t, 2 * TOK) for ref in (here_ref, got_ref) for t in range(TICKS)]
    far = [both_columns(ref, t, TOK) for ref in (far_ref, far_got_ref) for t in range(TICKS)]
    fill_right(core_ref, right_ref, near, far)
    for copy in copies:
        copy.wait()
    core = core_ref[0]
    for n in range(4):
        wide = pl.ds(pl.multiple_of(core * 1024 + n * 256, 256), 256)
        both = dot_tn(x_ref[:, :, wide].reshape(1024, 256), right_ref[...])
        query_ref[wide] = both[:, :256].astype(BF)
        pairs_ref[n * 256:(n + 1) * 256] = both[:, 256:].astype(BF)
    for n in range(4):
        wide = pl.ds(pl.multiple_of((1 - core) * 1024 + n * 256, 256), 256)
        query_ref[wide] = dot_tn(x_ref[:, :, wide].reshape(1024, 256), right_ref[:, :256]).astype(BF)


def columns(core, x, after, rights):
    return pl.pallas_call(
        columns_kernel,
        out_shape=(
            jax.ShapeDtypeStruct((HALF, 256), BF),
            jax.ShapeDtypeStruct((1024, 256), BF),
        ),
        in_specs=[pl.BlockSpec(memory_space=pltpu.SMEM)] + [HBM] * 2 + [VMEM] * 4,
        out_specs=(VMEM, VMEM),
        scratch_shapes=[
            pltpu.VMEM((16, 64, HALF), BF),
            pltpu.VMEM((1024, 512), BF),
            pltpu.SemaphoreType.DMA((2,)),
        ],
        cost_estimate=pl.CostEstimate(flops=1000, bytes_accessed=1000, transcendentals=0),
        compiler_params=params(58),
    )(core.reshape(1), x, after, *rights)


def output_kernel(
    core_ref, x_hbm, near_hbm, far_hbm, here, got, far,
    out_ref, g_ref, right_ref, second_ref, second_right, sems,
):
    copies = [
        pltpu.make_async_copy(x_hbm.at[:, 32:48], g_ref.at[:, :16], sems.at[0]),
        pltpu.make_async_copy(x_hbm.at[:, 80:], g_ref.at[:, 16:], sems.at[1]),
        pltpu.make_async_copy(near_hbm, second_ref.at[:2 * TOK], sems.at[2]),
        pltpu.make_async_copy(far_hbm, second_ref.at[2 * TOK:], sems.at[3]),
    ]
    for copy in copies:
        copy.start()

    near_rows = [lambda at, ref=ref: ref[0, at:at + 16, :256] for ref in (here, got)]
    far_rows = [lambda at, s=s: far[s, 0, at:at + 16] for s in range(2)]
    fill_right(core_ref, right_ref, near_rows, far_rows)
    for n, ref in enumerate((here, got)):
        second_right[n * TOK:(n + 1) * TOK] = ref[1, :, :256]
    for s in range(2):
        second_right[(2 + s) * TOK:(3 + s) * TOK] = far[s, 1]
    for copy in copies:
        copy.wait()
    for j in range(8):
        wide = pl.ds(j * 256, 256)
        out = dot_tn(g_ref[:, :, wide].reshape(512, 256), right_ref[...])
        out += dot_tn(second_ref[:, wide], second_right[...])
        out_ref[wide] = out.astype(BF)


def output_columns(core, x, near, far, attended):
    return pl.pallas_call(
        output_kernel,
        out_shape=jax.ShapeDtypeStruct((HALF, 256), BF),
        in_specs=[pl.BlockSpec(memory_space=pltpu.SMEM)] + [HBM] * 3 + [VMEM] * 3,
        out_specs=VMEM,
        scratch_shapes=[
            pltpu.VMEM((16, 32, HALF), BF),
            pltpu.VMEM((512, 256), BF),
            pltpu.VMEM((512, HALF), BF),
            pltpu.VMEM((512, 256), BF),
            pltpu.SemaphoreType.DMA((4,)),
        ],
        cost_estimate=pl.CostEstimate(flops=1000, bytes_accessed=1000, transcendentals=0),
        compiler_params=params(58),
    )(core.reshape(1), x, near, far, *attended)


def on_device(weight_q, weight_kv, weight_o, section_inputs, saved_q, saved_kv, out_grads):
    position = lax.axis_index("section")
    column = lax.axis_index("tensor")
    core = column % 2
    z_low = column // 2 % 2
    half = (position >= 8).astype(jnp.int32)
    next_half = (position + 2 * core - 1 >= 8).astype(jnp.int32)
    w_q, w_kv, w_o = weight_q[0], weight_kv[0], weight_o[0]
    inputs = section_inputs[:, :, 0]
    grads = out_grads[:, 0]

    def pick(x, index):
        return lax.dynamic_index_in_dim(x, index, 0, keepdims=False)

    def features_of(x, which):
        return lax.dynamic_slice_in_dim(x, which * HALF, HALF, x.ndim - 1)

    rows = exchange16(first_blocks(grads, inputs))

    wo_far = swap_core(w_o)
    queries = saved_q[:, :, 0]
    queries = jnp.concatenate([pick(queries, core), swap_core(pick(queries, 1 - core))], -1)
    wq_far = swap_core(w_q)
    pairs = pick(saved_kv[:, :, 0], core)
    attention, attended = attend(queries, pairs)
    chip = (column // 2).astype(jnp.int32)
    sent, held = split_rows(half, chip, rows)
    att_m = mirror(attended)
    near_o, near_q, near_kv = swap_core(wo_far), swap_core(wq_far), swap_core(w_kv)
    rows, sent, held, wo_far, wq_far, near_o, near_q, near_kv, attention = together(
        rows, sent, held, wo_far, wq_far, near_o, near_q, near_kv, attention
    )

    def both_chips(p):
        return (p.astype(F32) + swap_z(p).astype(F32)).astype(BF)

    def block(x, at):
        return x[at * TOK:(at + 1) * TOK]

    def held_near(x):
        return pltpu.with_memory_space_constraint(x, pltpu.VMEM)

    w_o, wo_far, w_q, wq_far, w_kv = map(held_near, (near_o, wo_far, near_q, wq_far, near_kv))

    terms, parts_0 = back(
        0, rows, w_o, wo_far, w_q, wq_far, w_kv, queries, pairs, attention
    )
    parts_0, sent = together(parts_0, sent)
    terms, att_m = together(terms, att_m)
    terms_0 = exchange8(terms.reshape(8, 16, WIDTH))
    got = mirror(sent)
    terms_0, got = together(terms_0, got)

    grad_in_0, blocks_0 = finish(0, chip, terms_0, rows)
    grad_rows = next_section(grad_in_0)
    sum_0 = both_chips(block(parts_0, 2))
    grad_half = next_mirror(
        lax.dynamic_slice_in_dim(grad_in_0, (1 - next_half) * HALF, HALF, 1)
    )

    spread_1 = jnp.concatenate([grad_rows, grad_half], 1)
    spread_1 = jnp.broadcast_to(spread_1[None], (8,) + spread_1.shape)
    x_rows = jnp.concatenate([held, got], 0)
    spread_1, parts_0, sum_0, x_rows = together(spread_1, parts_0, sum_0, x_rows)
    full_1 = exchange8(spread_1)
    x_all = gather16(x_rows)
    terms, parts_1 = back(
        1, full_1, w_o, wo_far, w_q, wq_far, w_kv, queries, pairs, attention
    )
    sum_1 = both_chips(block(parts_1, 2))
    terms, sum_1 = together(terms, sum_1)
    terms_1 = exchange8(terms.reshape(8, 16, WIDTH))
    here = jnp.stack(
        [jnp.concatenate([parts_0[:2 * TOK], sum_0], 0), jnp.concatenate([parts_1[:2 * TOK], sum_1], 0)]
    )
    late_m = mirror(here)
    far_here = swap_core(here[:, TOK:])

    att_far = swap_core(jnp.stack([attended[..., 256:], att_m[..., 256:]]))
    g_near = jnp.concatenate(
        [lax.dynamic_slice_in_dim(full_1, half * HALF, HALF, 2), full_1[:, :, WIDTH:]], 0
    ).reshape(256, HALF)
    g_far = swap_core(g_near)
    terms_1, x_all, g_far = together(terms_1, x_all, g_far)

    after, blocks_1 = finish(1, chip, terms_1, rows, grad_rows, blocks_0)
    out = exchange16(blocks_1)[:, :TICKS * 16]
    after, x_all = together(after, x_all)
    x_all = x_all.reshape(16, 96, HALF)
    grad_output = output_columns(core, x_all, g_near, g_far, [attended, att_m, att_far])
    grad_output, late_m = together(grad_output, late_m)
    far_late = swap_core(late_m[:, TOK:])
    grad_query, acc_kv = columns(core, x_all, after, [here, late_m, far_here, far_late])
    kept = lax.dynamic_slice_in_dim(acc_kv, half * 512, 512, 0)
    given = lax.dynamic_slice_in_dim(acc_kv, (1 - half) * 512, 512, 0)
    taken = send(given, lambda s, c: (15 - s, c) if c // 2 % 2 == s // 8 else None)
    grad_kv = jnp.where(z_low == half, kept, taken)

    input_grads = out.reshape(8, 2, TICKS, 16, 256).transpose(1, 2, 0, 3, 4)
    input_grads = input_grads.reshape(2, TICKS, 1, TOK, 256)
    return (input_grads, grad_query[None], grad_kv[None], grad_output[None])


def solution(mesh):
    placed = (
        P("section", None, "tensor"),
        P("section", None, "tensor"),
        P("section", None, "tensor"),
        P(None, None, "section", None, "tensor"),
        P(None, None, "section", None, "tensor"),
        P(None, None, "section", None, "tensor"),
        P(None, "section", None, "tensor"),
    )
    return jax.shard_map(
        on_device,
        mesh=mesh,
        in_specs=placed,
        out_specs=(
            P(None, None, "section", None, "tensor"),
            P("section", None, "tensor"),
            P("section", None, "tensor"),
            P("section", None, "tensor"),
        ),
        check_vma=False,
    )
```

```python
import functools

import jax
import jax.numpy as jnp
from jax import lax
from jax.experimental import pallas as pl
from jax.experimental.pallas import tpu as pltpu
from jax.sharding import PartitionSpec as P

HD = 128
TICKS = 2
TOK = 128
WIDTH = 4096
HALF = WIDTH // 2
SCALE = HD ** (-0.5)
BF = jnp.bfloat16
F32 = jnp.float32

SAME_CORE = [[core + 2 * chip for chip in range(8)] for core in range(2)]
VMEM = pl.BlockSpec(memory_space=pltpu.VMEM)
HBM = pl.BlockSpec(memory_space=pl.ANY)


def send(x, route):
    pairs = []
    for section in range(16):
        for tensor in range(16):
            target = route(section, tensor)
            if target is not None:
                pairs.append((section * 16 + tensor, target[0] * 16 + target[1]))
    return lax.ppermute(x, ("section", "tensor"), pairs)


def swap_core(x):
    return lax.ppermute(x, "tensor", [(i, i ^ 1) for i in range(16)])


def swap_z(x):
    return lax.ppermute(x, "tensor", [(i, i ^ 2) for i in range(16)])


def swap_y(x, k):
    return lax.ppermute(x, "tensor", [(i, i ^ 4 * k) for i in range(16)])


def mirror(x):
    return lax.ppermute(x, "section", [(i, 15 - i) for i in range(16)])


def next_section(x):
    def route(s, c):
        target = s - 1 if c % 2 == 0 else s + 1
        return (target, c) if 0 <= target < 16 else None

    return send(x, route)


def next_mirror(x):
    def route(s, c):
        target = s - 1 if c % 2 == 0 else s + 1
        return (15 - target, c) if 0 <= target < 16 else None

    return send(x, route)


def exchange8(x):
    return lax.all_to_all(x, "tensor", 0, 0, axis_index_groups=SAME_CORE, tiled=True)


def exchange16(x):
    return lax.all_to_all(x, "tensor", 0, 0, tiled=True)


def gather16(x):
    return lax.all_gather(x, "tensor", axis=0, tiled=True)


def dot(a, b):
    return jnp.dot(a, b, preferred_element_type=F32)


def dot_nt(a, b):
    return lax.dot_general(a, b, (((1,), (1,)), ((), ())), preferred_element_type=F32)


def dot_tn(a, b):
    return lax.dot_general(a, b, (((0,), (0,)), ((), ())), preferred_element_type=F32)


def together(*values):
    return lax.optimization_barrier(values)


def params(mib):
    return pltpu.CompilerParams(vmem_limit_bytes=mib * 2**20)


def first_kernel(grads_ref, inputs_ref, out_ref):
    for m in range(8):
        for r in range(2):
            out_ref[2 * m + r, :TOK] = grads_ref[r]
            for t in range(TICKS):
                at = TOK + 16 * t
                out_ref[2 * m + r, at:at + 16] = inputs_ref[r, t, m * 16:m * 16 + 16]


def first_blocks(grads, inputs):
    return pl.pallas_call(
        first_kernel,
        out_shape=jax.ShapeDtypeStruct((16, TOK + 32, 256), BF),
        in_specs=[VMEM] * 2,
        out_specs=VMEM,
        compiler_params=params(16),
    )(grads, inputs)


def attend_kernel(q_ref, kv_ref, attention_ref, attended_ref):
    rows = lax.broadcasted_iota(jnp.int32, (TOK, TOK), 0)
    columns = lax.broadcasted_iota(jnp.int32, (TOK, TOK), 1)
    causal = rows >= columns
    for t in range(TICKS):
        keys = kv_ref[t, :, :HD]
        values = kv_ref[t, :, HD:]
        for a in range(4):
            head = slice(a * HD, (a + 1) * HD)
            scores = jnp.where(causal, dot_nt(q_ref[t, :, head], keys) * SCALE, -1e30)
            weights = jnp.exp(scores - jnp.max(scores, axis=-1, keepdims=True))
            weights = weights / jnp.sum(weights, axis=-1, keepdims=True)
            attention_ref[t, a] = weights
            attended_ref[t, :, head] = dot(weights.astype(BF), values).astype(BF)


def attend(queries, pairs):
    return pl.pallas_call(
        attend_kernel,
        out_shape=(
            jax.ShapeDtypeStruct((TICKS, 4, TOK, TOK), F32),
            jax.ShapeDtypeStruct((TICKS, TOK, 4 * HD), BF),
        ),
        in_specs=[VMEM] * 2,
        out_specs=(VMEM, VMEM),
        compiler_params=params(16),
    )(queries, pairs)


CHUNKS = 4
DEEP = WIDTH // CHUNKS


def back_kernel(
    tick,
    g_hbm, wo_own_ref, wo_far_ref, wq_own_ref, wq_far_ref, wkv_ref, q_ref, kv_ref, attention_ref,
    terms_ref, parts_ref,
    g_ref, grad_heads, heads, g_sems,
):
    own_ref, far_ref, pairs_ref = (parts_ref.at[pl.ds(n * TOK, TOK)] for n in range(3))
    copies = []
    for c in range(CHUNKS):
        if tick == 0:
            part = pl.ds(c * 16 // CHUNKS, 16 // CHUNKS)
            copies.append(pltpu.make_async_copy(g_hbm.at[part, :TOK], g_ref.at[part], g_sems.at[c]))
        else:
            deep = pl.ds(c * DEEP, DEEP)
            copies.append(pltpu.make_async_copy(g_hbm.at[:, :, deep], g_ref.at[:, :, deep], g_sems.at[c]))
    for copy in copies:
        copy.start()
    for a in range(4):
        heads[a * TOK:(a + 1) * TOK] = q_ref[tick, :, a * HD:(a + 1) * HD]
    own = jnp.zeros((TOK, 256), F32)
    far = jnp.zeros((TOK, 256), F32)
    for c in range(CHUNKS):
        copies[c].wait()
        if tick == 0:
            for block in range(c * 16 // CHUNKS, (c + 1) * 16 // CHUNKS):
                deep = pl.ds(block * 256, 256)
                own += dot(g_ref[block], wo_own_ref[deep])
                far += dot(g_ref[block], wo_far_ref[deep])
        else:
            deep = pl.ds(c * DEEP, DEEP)
            part = g_ref[:, :, deep].reshape(TOK, DEEP)
            own += dot(part, wo_own_ref[deep])
            far += dot(part, wo_far_ref[deep])
    keys = kv_ref[tick, :, :HD]
    values = kv_ref[tick, :, HD:]
    for a in range(4):
        side = own if a < 2 else far
        grad_heads[a * TOK:(a + 1) * TOK] = side[:, a % 2 * HD:(a % 2 + 1) * HD].astype(BF)
    grad_probs = dot_nt(grad_heads[...], values)
    attention = attention_ref[tick].reshape(4 * TOK, TOK)
    row_delta = jnp.sum(attention * grad_probs, axis=-1, keepdims=True)
    grad_scores = (attention * (grad_probs - row_delta) * SCALE).astype(BF)
    query_grad = dot(grad_scores, keys).astype(BF)
    for a in range(4):
        target = own_ref if a < 2 else far_ref
        target[:, a % 2 * HD:(a % 2 + 1) * HD] = query_grad[a * TOK:(a + 1) * TOK]
    pairs_ref[:, :HD] = dot_tn(grad_scores, heads[...]).astype(BF)
    pairs_ref[:, HD:] = dot_tn(attention.astype(BF), grad_heads[...]).astype(BF)
    for n in range(8):
        wide = pl.ds(n * 512, 512)
        out = dot_nt(own_ref[...], wq_own_ref[wide]) + dot_nt(far_ref[...], wq_far_ref[wide])
        out = out + dot_nt(pairs_ref[...], wkv_ref[wide])
        terms_ref[:, wide] = out.astype(BF)


def back(tick, grads, wo_own, wo_far, wq_own, wq_far, w_kv, queries, pairs, attention):
    return pl.pallas_call(
        functools.partial(back_kernel, tick),
        out_shape=(
            jax.ShapeDtypeStruct((TOK, WIDTH), BF),
            jax.ShapeDtypeStruct((3 * TOK, 256), BF),
        ),
        in_specs=[HBM] + [VMEM] * 8,
        out_specs=(VMEM, VMEM),
        scratch_shapes=[
            pltpu.VMEM((16, TOK, 256) if tick == 0 else (8, 16, WIDTH), BF),
            pltpu.VMEM((4 * TOK, HD), BF),
            pltpu.VMEM((4 * TOK, HD), BF),
            pltpu.SemaphoreType.DMA((CHUNKS,)),
        ],
        compiler_params=params(24),
    )(grads, wo_own, wo_far, wq_own, wq_far, w_kv, queries, pairs, attention)


def finish_kernel(first, tick, chip_ref, terms_ref, rows_ref, grad_ref, before_ref, out_ref, blocks_ref, kept):
    x_at = TOK + 16 * tick
    here = pl.ds(pl.multiple_of(chip_ref[0] * 16, 16), 16)
    squares = jnp.zeros((16, 256), F32)
    products = jnp.zeros((16, 256), F32)
    for j in range(16):
        wide = pl.ds(j * 256, 256)
        x = rows_ref[j, x_at:x_at + 16].astype(F32)
        total = terms_ref[0, :, wide].astype(F32)
        for m in range(1, 8):
            total += terms_ref[m, :, wide].astype(F32)
        kept[:, wide] = total
        squares += x * x
        products += total * x
    inverse = lax.rsqrt(jnp.sum(squares, axis=-1, keepdims=True) / WIDTH + 1e-06)
    shift = jnp.sum(products, axis=-1, keepdims=True) * inverse * inverse / WIDTH
    for j in range(16):
        wide = pl.ds(j * 256, 256)
        x = rows_ref[j, x_at:x_at + 16].astype(F32)
        before = rows_ref[j, here] if first else grad_ref[:, wide]
        out = before.astype(F32) + inverse * (kept[:, wide] - x * shift)
        out = out.astype(BF)
        out_ref[:, wide] = out
        if first:
            blocks_ref[j] = out
        else:
            blocks_ref[j, :16] = before_ref[j]
            blocks_ref[j, 16:] = out


def finish(tick, chip, terms, rows, grad_rows=None, blocks=None):
    first = tick == 0
    operands = (chip.reshape(1), terms, rows) + (() if first else (grad_rows, blocks))

    def kernel(*refs):
        if first:
            finish_kernel(first, tick, *refs[:3], None, None, *refs[3:])
        else:
            finish_kernel(first, tick, *refs)

    return pl.pallas_call(
        kernel,
        out_shape=(
            jax.ShapeDtypeStruct((16, WIDTH), BF),
            jax.ShapeDtypeStruct((16, 16 if first else 32, 256), BF),
        ),
        in_specs=[pl.BlockSpec(memory_space=pltpu.SMEM)] + [VMEM] * (len(operands) - 1),
        out_specs=(VMEM, VMEM),
        scratch_shapes=[pltpu.VMEM((16, WIDTH), F32)],
        compiler_params=params(16),
    )(*operands)


def rows_kernel(half_ref, chip_ref, rows_ref, sent_ref, held_ref):
    rows = 32
    squares = jnp.zeros((rows, 256), F32)
    for j in range(16):
        x = rows_ref[j, TOK:].astype(F32)
        squares += x * x
    inverse = lax.rsqrt(jnp.sum(squares, axis=-1, keepdims=True) / WIDTH + 1e-06)
    half = half_ref[0]
    here = pl.ds(pl.multiple_of(chip_ref[0] * 16, 16), 16)
    for j in range(8):
        wide = pl.ds(j * 256, 256)
        near, far = half * 8 + j, (1 - half) * 8 + j
        held_ref[:rows, wide] = (rows_ref[near, TOK:].astype(F32) * inverse).astype(BF)
        sent_ref[:rows, wide] = (rows_ref[far, TOK:].astype(F32) * inverse).astype(BF)
        sent_ref[rows:, wide] = rows_ref[far, here]
        held_ref[rows:, wide] = rows_ref[near, here]


def split_rows(half, chip, rows):
    return pl.pallas_call(
        rows_kernel,
        out_shape=(
            jax.ShapeDtypeStruct((48, HALF), BF),
            jax.ShapeDtypeStruct((48, HALF), BF),
        ),
        in_specs=[pl.BlockSpec(memory_space=pltpu.SMEM)] * 2 + [VMEM],
        out_specs=(VMEM, VMEM),
        compiler_params=params(16),
    )(half.reshape(1), chip.reshape(1), rows)


def fill_right(core_ref, right_ref, near, far):
    core = core_ref[0]
    for side, sources in enumerate((near, far)):
        direction = core if side == 0 else 1 - core
        for m in range(8):
            for group, source in enumerate(sources):
                at = (2 * m + direction) * 16 * len(sources) + group * 16
                value = source(m * 16)
                right_ref[pl.ds(pl.multiple_of(at, 16), 16)] = value


def columns_kernel(
    core_ref, x_hbm, after_hbm, here_ref, got_ref, far_ref, far_got_ref,
    query_ref, pairs_ref, x_ref, right_ref, sems,
):
    copies = [
        pltpu.make_async_copy(x_hbm.at[:, :32], x_ref.at[:, :32], sems.at[0]),
        pltpu.make_async_copy(x_hbm.at[:, 48:80], x_ref.at[:, 32:], sems.at[1]),
    ]
    for copy in copies:
        copy.start()

    def both_columns(ref, t, pairs_at):
        return lambda at: jnp.concatenate(
            [ref[t, at:at + 16], ref[t, pairs_at + at:pairs_at + at + 16]], -1
        )

    near = [both_columns(ref, t, 2 * TOK) for ref in (here_ref, got_ref) for t in range(TICKS)]
    far = [both_columns(ref, t, TOK) for ref in (far_ref, far_got_ref) for t in range(TICKS)]
    fill_right(core_ref, right_ref, near, far)
    for copy in copies:
        copy.wait()
    core = core_ref[0]
    for n in range(4):
        wide = pl.ds(pl.multiple_of(core * 1024 + n * 256, 256), 256)
        both = dot_tn(x_ref[:, :, wide].reshape(1024, 256), right_ref[...])
        query_ref[wide] = both[:, :256].astype(BF)
        pairs_ref[n * 256:(n + 1) * 256] = both[:, 256:].astype(BF)
    for n in range(4):
        wide = pl.ds(pl.multiple_of((1 - core) * 1024 + n * 256, 256), 256)
        query_ref[wide] = dot_tn(x_ref[:, :, wide].reshape(1024, 256), right_ref[:, :256]).astype(BF)


def columns(core, x, after, rights):
    return pl.pallas_call(
        columns_kernel,
        out_shape=(
            jax.ShapeDtypeStruct((HALF, 256), BF),
            jax.ShapeDtypeStruct((1024, 256), BF),
        ),
        in_specs=[pl.BlockSpec(memory_space=pltpu.SMEM)] + [HBM] * 2 + [VMEM] * 4,
        out_specs=(VMEM, VMEM),
        scratch_shapes=[
            pltpu.VMEM((16, 64, HALF), BF),
            pltpu.VMEM((1024, 512), BF),
            pltpu.SemaphoreType.DMA((2,)),
        ],
        cost_estimate=pl.CostEstimate(flops=1000, bytes_accessed=1000, transcendentals=0),
        compiler_params=params(58),
    )(core.reshape(1), x, after, *rights)


def output_kernel(
    core_ref, x_hbm, near_hbm, far_hbm, here, got, far,
    out_ref, g_ref, right_ref, second_ref, second_right, sems,
):
    copies = [
        pltpu.make_async_copy(x_hbm.at[:, 32:48], g_ref.at[:, :16], sems.at[0]),
        pltpu.make_async_copy(x_hbm.at[:, 80:], g_ref.at[:, 16:], sems.at[1]),
        pltpu.make_async_copy(near_hbm, second_ref.at[:2 * TOK], sems.at[2]),
        pltpu.make_async_copy(far_hbm, second_ref.at[2 * TOK:], sems.at[3]),
    ]
    for copy in copies:
        copy.start()

    near_rows = [lambda at, ref=ref: ref[0, at:at + 16, :256] for ref in (here, got)]
    far_rows = [lambda at, s=s: far[s, 0, at:at + 16] for s in range(2)]
    fill_right(core_ref, right_ref, near_rows, far_rows)
    for n, ref in enumerate((here, got)):
        second_right[n * TOK:(n + 1) * TOK] = ref[1, :, :256]
    for s in range(2):
        second_right[(2 + s) * TOK:(3 + s) * TOK] = far[s, 1]
    for copy in copies:
        copy.wait()
    for j in range(8):
        wide = pl.ds(j * 256, 256)
        out = dot_tn(g_ref[:, :, wide].reshape(512, 256), right_ref[...])
        out += dot_tn(second_ref[:, wide], second_right[...])
        out_ref[wide] = out.astype(BF)


def output_columns(core, x, near, far, attended):
    return pl.pallas_call(
        output_kernel,
        out_shape=jax.ShapeDtypeStruct((HALF, 256), BF),
        in_specs=[pl.BlockSpec(memory_space=pltpu.SMEM)] + [HBM] * 3 + [VMEM] * 3,
        out_specs=VMEM,
        scratch_shapes=[
            pltpu.VMEM((16, 32, HALF), BF),
            pltpu.VMEM((512, 256), BF),
            pltpu.VMEM((512, HALF), BF),
            pltpu.VMEM((512, 256), BF),
            pltpu.SemaphoreType.DMA((4,)),
        ],
        cost_estimate=pl.CostEstimate(flops=1000, bytes_accessed=1000, transcendentals=0),
        compiler_params=params(58),
    )(core.reshape(1), x, near, far, *attended)


def on_device(weight_q, weight_kv, weight_o, section_inputs, saved_q, saved_kv, out_grads):
    position = lax.axis_index("section")
    column = lax.axis_index("tensor")
    core = column % 2
    z_low = column // 2 % 2
    half = (position >= 8).astype(jnp.int32)
    next_half = (position + 2 * core - 1 >= 8).astype(jnp.int32)
    w_q, w_kv, w_o = weight_q[0], weight_kv[0], weight_o[0]
    inputs = section_inputs[:, :, 0]
    grads = out_grads[:, 0]

    def pick(x, index):
        return lax.dynamic_index_in_dim(x, index, 0, keepdims=False)

    def features_of(x, which):
        return lax.dynamic_slice_in_dim(x, which * HALF, HALF, x.ndim - 1)

    rows = exchange16(first_blocks(grads, inputs))

    wo_far = swap_core(w_o)
    queries = saved_q[:, :, 0]
    queries = jnp.concatenate([pick(queries, core), swap_core(pick(queries, 1 - core))], -1)
    wq_far = swap_core(w_q)
    pairs = pick(saved_kv[:, :, 0], core)
    attention, attended = attend(queries, pairs)
    chip = (column // 2).astype(jnp.int32)
    sent, held = split_rows(half, chip, rows)
    att_m = mirror(attended)
    near_o, near_q, near_kv = swap_core(wo_far), swap_core(wq_far), swap_core(w_kv)
    rows, sent, held, wo_far, wq_far, near_o, near_q, near_kv, attention = together(
        rows, sent, held, wo_far, wq_far, near_o, near_q, near_kv, attention
    )

    def both_chips(p):
        return (p.astype(F32) + swap_z(p).astype(F32)).astype(BF)

    def block(x, at):
        return x[at * TOK:(at + 1) * TOK]

    def held_near(x):
        return pltpu.with_memory_space_constraint(x, pltpu.VMEM)

    w_o, wo_far, w_q, wq_far, w_kv = map(held_near, (near_o, wo_far, near_q, wq_far, near_kv))

    terms, parts_0 = back(
        0, rows, w_o, wo_far, w_q, wq_far, w_kv, queries, pairs, attention
    )
    parts_0, sent = together(parts_0, sent)
    terms, att_m = together(terms, att_m)
    terms_0 = exchange8(terms.reshape(8, 16, WIDTH))
    got = mirror(sent)
    terms_0, got = together(terms_0, got)

    grad_in_0, blocks_0 = finish(0, chip, terms_0, rows)
    grad_rows = next_section(grad_in_0)
    sum_0 = both_chips(block(parts_0, 2))
    grad_half = next_mirror(
        lax.dynamic_slice_in_dim(grad_in_0, (1 - next_half) * HALF, HALF, 1)
    )

    spread_1 = jnp.concatenate([grad_rows, grad_half], 1)
    spread_1 = jnp.broadcast_to(spread_1[None], (8,) + spread_1.shape)
    x_rows = jnp.concatenate([held, got], 0)
    spread_1, parts_0, sum_0, x_rows = together(spread_1, parts_0, sum_0, x_rows)
    full_1 = exchange8(spread_1)
    x_all = gather16(x_rows)
    terms, parts_1 = back(
        1, full_1, w_o, wo_far, w_q, wq_far, w_kv, queries, pairs, attention
    )
    sum_1 = both_chips(block(parts_1, 2))
    terms, sum_1 = together(terms, sum_1)
    terms_1 = exchange8(terms.reshape(8, 16, WIDTH))
    here = jnp.stack(
        [jnp.concatenate([parts_0[:2 * TOK], sum_0], 0), jnp.concatenate([parts_1[:2 * TOK], sum_1], 0)]
    )
    late_m = mirror(here)
    far_here = swap_core(here[:, TOK:])

    att_far = swap_core(jnp.stack([attended[..., 256:], att_m[..., 256:]]))
    g_near = jnp.concatenate(
        [lax.dynamic_slice_in_dim(full_1, half * HALF, HALF, 2), full_1[:, :, WIDTH:]], 0
    ).reshape(256, HALF)
    g_far = swap_core(g_near)
    terms_1, x_all, g_far = together(terms_1, x_all, g_far)

    after, blocks_1 = finish(1, chip, terms_1, rows, grad_rows, blocks_0)
    out = exchange16(blocks_1)
    after, x_all = together(after, x_all)
    x_all = x_all.reshape(16, 96, HALF)
    grad_output = output_columns(core, x_all, g_near, g_far, [attended, att_m, att_far])
    grad_output, late_m = together(grad_output, late_m)
    far_late = swap_core(late_m[:, TOK:])
    grad_query, acc_kv = columns(core, x_all, after, [here, late_m, far_here, far_late])
    kept = lax.dynamic_slice_in_dim(acc_kv, half * 512, 512, 0)
    given = lax.dynamic_slice_in_dim(acc_kv, (1 - half) * 512, 512, 0)
    taken = send(given, lambda s, c: (15 - s, c) if c // 2 % 2 == s // 8 else None)
    grad_kv = jnp.where(z_low == half, kept, taken)

    input_grads = out.reshape(8, 2, TICKS, 16, 256).transpose(1, 2, 0, 3, 4)
    input_grads = input_grads.reshape(2, TICKS, 1, TOK, 256)
    return (input_grads, grad_query[None], grad_kv[None], grad_output[None])


def solution(mesh):
    placed = (
        P("section", None, "tensor"),
        P("section", None, "tensor"),
        P("section", None, "tensor"),
        P(None, None, "section", None, "tensor"),
        P(None, None, "section", None, "tensor"),
        P(None, None, "section", None, "tensor"),
        P(None, "section", None, "tensor"),
    )
    return jax.shard_map(
        on_device,
        mesh=mesh,
        in_specs=placed,
        out_specs=(
            P(None, None, "section", None, "tensor"),
            P("section", None, "tensor"),
            P("section", None, "tensor"),
            P("section", None, "tensor"),
        ),
        check_vma=False,
    )
```
